256 devices in a mesh: dir: 2 (over core), seq: 128 (over y, z, x).
Axes of the slice: x: 4, y: 4, z: 8, core: 2. Of those that a mesh axis runs over, the one named last changes fastest.
Arguments:
- queries: bfloat16 [2, 4, 8192, 4096], P('dir', None, 'seq'), may hold values from -35 to 35
- key_states: bfloat16 [2, 4, 8192, 4096], P('dir', None, 'seq'), may hold values from -6 to 6
- value_vectors: bfloat16 [2, 4, 8192, 4096], P('dir', None, 'seq'), may hold values from -6 to 6
- hypothesis_lengths: int32 [4, 512], replicated, may hold values from 1 to 256, 8192 in all within a row
- join_weight: bfloat16 [8192, 2, 1024], P('seq', None, 'dir'), may hold values from -0.0625 to 0.0625
Outputs:
- joined: bfloat16 [4, 8192, 1024], P(None, 'seq', 'dir')
The draws below stay inside these ranges and needn't reach their ends.
All inputs are finite; a program needn't handle non-finite values.
Results may differ from the reference program's by a relative error of at most 0.0072.
Values may be sent and summed in bfloat16 or wider, within the bound.
No kernel may reach another device: no remote copies, remote signals or barrier semaphores. Data moves between devices by JAX's collectives and lax.ppermute only.
A program may use at most 128 MiB of HBM per device.

```python
import math
import jax
import jax.numpy as jnp
import numpy as np
from jax import lax

MODEL_WIDTH = 4096
ATTENTION_HEADS = 32
PACKED_ROWS = 4
GROUP_HEADS = 1
JOIN_UNITS = 1024
LONGEST_TOKENS = 256
ROW_POSITIONS = 8192
ROW_HYPOTHESES = 512


def draw_queries(key, part):
    key = jax.random.fold_in(key, 11)
    array_shape = (2, PACKED_ROWS, ROW_POSITIONS, MODEL_WIDTH)
    values = jax.random.truncated_normal(key, -6.0, 6.0, array_shape, jnp.float32)
    return values.astype(jnp.bfloat16)


def draw_key_states(key, part):
    key = jax.random.fold_in(key, 23)
    array_shape = (2, PACKED_ROWS, ROW_POSITIONS, MODEL_WIDTH)
    values = jax.random.truncated_normal(key, -6.0, 6.0, array_shape, jnp.float32)
    return values.astype(jnp.bfloat16)


def block_levels(key, shape, pieces, low, largest):
    gain, own = 1.0, jax.random.fold_in(key, 6)
    for axis_at, shards_of in pieces:
        heights = jnp.exp(jax.random.uniform(jax.random.fold_in(own, axis_at), (shards_of,), jnp.float32, low / len(pieces), largest / len(pieces)))
        gain = gain * jnp.repeat(heights, shape[axis_at] // shards_of).reshape([-1 if axis == axis_at else 1 for axis in range(len(shape))])
    return gain


def profile(amount, total, limit, lean):
    weights = [(1 << 20) // math.isqrt(grade ** lean) + 1 for grade in range(2, amount + 1)]
    spare, holding = total - limit - (amount - 1), [1] * (amount - 1)
    while spare > 0:
        movable = [i for i in range(amount - 1) if holding[i] < limit]
        whole, left = sum([weights[i] for i in movable]), spare
        for i in movable:
            extra = min(limit - holding[i], max(1, left * weights[i] // whole), spare)
            holding[i] = holding[i] + extra
            spare = spare - extra
    return np.array([limit] + holding)


def ragged_sizes(rng, number_of, total, reach, lean):
    if number_of == 2:
        one = jax.random.randint(rng, (), max(1, total - reach), min(reach, total - 1) + 1)
        return jnp.stack([one, total - one])
    lengths = jnp.asarray(profile(number_of, total, reach, lean), jnp.int32)
    pairs = (number_of - 1) // 2
    donor, taker = lengths[1:1 + 2 * pairs:2], lengths[2:2 + 2 * pairs:2]
    room = jnp.minimum(donor - 1, reach - taker)
    shifted = jax.random.randint(jax.random.fold_in(rng, 1), (pairs,), 0, 1 << 20) % (room + 1)
    lengths = lengths.at[1:1 + 2 * pairs:2].set(donor - shifted).at[2:2 + 2 * pairs:2].set(taker + shifted)
    return lengths[jax.random.permutation(jax.random.fold_in(rng, 2), number_of)]


def normal_values(rng, dims, scale, most, pieces=(), held_as=jnp.bfloat16):
    entries = scale * jax.random.normal(rng, dims, jnp.float32)
    if pieces:
        entries = entries * block_levels(rng, dims, pieces, -0.22, 0.18)
    return jnp.clip(entries, -most, most).astype(held_as)


def setup_inputs(seed: int = 0) -> dict:
    key_of = jax.random.split(jax.random.key(seed), 6)
    queries = draw_queries(jax.random.fold_in(key_of[5], 71), 0)
    key_states = draw_key_states(jax.random.fold_in(key_of[5], 71), 0)
    value_vectors = normal_values(key_of[2], (2, PACKED_ROWS, ROW_POSITIONS, MODEL_WIDTH), 1.0, 6.0, ((0, 2), (2, 128)))
    hypothesis_lengths = jax.vmap(lambda own: ragged_sizes(own, ROW_HYPOTHESES, ROW_POSITIONS, LONGEST_TOKENS, 2))(jax.random.split(key_of[3], PACKED_ROWS)).reshape((PACKED_ROWS, ROW_HYPOTHESES)).astype(jnp.int32)
    join_weight = normal_values(key_of[4], (2 * MODEL_WIDTH, 2, JOIN_UNITS), (2 * MODEL_WIDTH) ** -0.5, 0.0625, ((0, 128), (2, 2)))
    return {"queries": queries, "key_states": key_states, "value_vectors": value_vectors, "hypothesis_lengths": hypothesis_lengths, "join_weight": join_weight}


def hypothesis_tables(length_list, row_len):
    length_list = length_list.astype(jnp.int32)
    ends = jnp.cumsum(length_list).astype(jnp.int32)
    starts = (ends - length_list).astype(jnp.int32)
    places = jnp.arange(row_len, dtype=jnp.int32)
    inside = (places[:, None] >= starts[None, :]) & (places[:, None] < ends[None, :])
    first = lax.optimization_barrier(jnp.sum(jnp.where(inside, starts[None, :], 0), axis=1)).astype(jnp.int32)
    after = lax.optimization_barrier(jnp.sum(jnp.where(inside, ends[None, :], 0), axis=1)).astype(jnp.int32)
    mirror = (first + after - 1 - places).astype(jnp.int32)
    return (first, mirror)

def attend_row(query_row, k_row, v_row, first):
    block_item = min(256, ROW_POSITIONS)
    token_span = min(block_item + LONGEST_TOKENS, ROW_POSITIONS)
    scale = 1.0 / math.sqrt(query_row.shape[2])

    def single_block(index):
        q_start = (index * block_item).astype(jnp.int32)
        k_start = jnp.maximum(q_start + block_item - token_span, 0).astype(jnp.int32)
        q_part = lax.dynamic_slice_in_dim(query_row, q_start, block_item, 0).astype(jnp.float32)
        k_part = lax.dynamic_slice_in_dim(k_row, k_start, token_span, 0).astype(jnp.float32)
        v_part = lax.dynamic_slice_in_dim(v_row, k_start, token_span, 0).astype(jnp.float32)
        scores = jnp.einsum('qhc,khc->hqk', q_part, k_part) * scale
        q_places = q_start + jnp.arange(block_item, dtype=jnp.int32)
        k_places = k_start + jnp.arange(token_span, dtype=jnp.int32)
        starts = lax.dynamic_slice_in_dim(first, q_start, block_item, 0)
        allowed = (k_places[None, :] >= starts[:, None]) & (k_places[None, :] <= q_places[:, None])
        scores = jnp.where(allowed[None], scores, jnp.float32(-1e+30))
        top = lax.optimization_barrier(jnp.max(scores, axis=2, keepdims=True))
        raised = jnp.exp(scores - top)
        weights = (raised / lax.optimization_barrier(jnp.sum(raised, axis=2, keepdims=True))).astype(jnp.bfloat16)
        weights = lax.optimization_barrier(weights).astype(jnp.float32)
        return jnp.einsum('hqk,khc->qhc', weights, v_part).astype(jnp.bfloat16)
    block_list = lax.map(single_block, jnp.arange(ROW_POSITIONS // block_item, dtype=jnp.int32))
    return block_list.reshape(ROW_POSITIONS, query_row.shape[1], query_row.shape[2])

def reference(queries, key_states, value_vectors, hypothesis_lengths, join_weight):
    head_width = MODEL_WIDTH // ATTENTION_HEADS
    leading_items, mirrored_items = jax.vmap(lambda length_list: hypothesis_tables(length_list, ROW_POSITIONS))(hypothesis_lengths)
    array_shape = (2 * PACKED_ROWS, ROW_POSITIONS, ATTENTION_HEADS, head_width)
    both_first = jnp.concatenate([leading_items, leading_items], axis=0)

    def per_row(items):
        return attend_row(items[0], items[1], items[2], items[3])
    context_vectors = lax.map(per_row, (queries.reshape(array_shape), key_states.reshape(array_shape), value_vectors.reshape(array_shape), both_first))
    context_vectors = context_vectors.reshape(2, PACKED_ROWS, ROW_POSITIONS, ATTENTION_HEADS, head_width)
    left_side = context_vectors[0]
    right_side = jnp.take_along_axis(context_vectors[1], mirrored_items[:, :, None, None], axis=1)
    feature_rows = jnp.stack([left_side, right_side], axis=3).reshape(PACKED_ROWS * ROW_POSITIONS, 2 * MODEL_WIDTH)
    matrix = join_weight.reshape(2 * MODEL_WIDTH, 2 * JOIN_UNITS)
    group_rows = 2 * GROUP_HEADS * head_width

    def append_group(grand_total, group):
        start = (group * group_rows).astype(jnp.int32)
        part_feat = lax.dynamic_slice_in_dim(feature_rows, start, group_rows, 1)
        part_weight = lax.dynamic_slice_in_dim(matrix, start, group_rows, 0)
        partial_value = jnp.dot(part_feat, part_weight, preferred_element_type=jnp.float32).astype(jnp.bfloat16)
        partial_value = lax.optimization_barrier(partial_value)
        return (grand_total + partial_value.astype(jnp.float32), None)
    grand_total, spare_tokens = lax.scan(append_group, jnp.zeros((PACKED_ROWS * ROW_POSITIONS, 2 * JOIN_UNITS), jnp.float32), jnp.arange(ATTENTION_HEADS // GROUP_HEADS, dtype=jnp.int32))
    joined = jax.nn.silu(grand_total[:, :JOIN_UNITS]) * grand_total[:, JOIN_UNITS:]
    return joined.astype(jnp.bfloat16).reshape(PACKED_ROWS, ROW_POSITIONS, JOIN_UNITS)
```

```python
import math

import jax
import jax.numpy as jnp
from jax import lax
from jax.experimental import pallas as pl
from jax.experimental.pallas import tpu as pltpu
from jax.sharding import Mesh
from jax.sharding import PartitionSpec as P

HEAD = 128
SPAN = 256
HALF = SPAN // 2
RINGS = 32
PER_STEP = 2
NT = (((1,), (1,)), ((), ()))
NN = (((1,), (0,)), ((), ()))


def dot(a, b, dims=NN):
    return lax.dot_general(a, b, dims, preferred_element_type=jnp.float32)


def one_hot(index, rows, columns):
    at = lax.broadcasted_iota(jnp.int32, (rows, columns), 1)
    return jnp.where(at == index, 1.0, 0.0).astype(jnp.bfloat16)


def tables(lengths, base):
    count = lengths.shape[1]
    order = jnp.arange(count, dtype=jnp.int32)
    upto = order[None, :] <= order[:, None]
    ends = jnp.sum(jnp.where(upto[None], lengths[:, None, :], 0), axis=2)
    starts = ends - lengths
    places = base + jnp.arange(SPAN, dtype=jnp.int32)
    at = places[None, :, None]
    inside = (at >= starts[:, None, :]) & (at < ends[:, None, :])
    first = jnp.sum(jnp.where(inside, starts[:, None, :], 0), axis=2) - base
    end = jnp.sum(jnp.where(inside, ends[:, None, :], 0), axis=2) - base
    return first, end


def attend_kernel(edge_ref, low_ref, q_ref, own_ref, before_ref, out_ref, ahead_ref, back_ref, bias):
    factor = math.log2(math.e) / math.sqrt(HEAD)
    wide = SPAN + HALF

    @pl.when(pl.program_id(0) == 0)
    def _():
        for part in range(2):
            key = lax.broadcasted_iota(jnp.int32, (HALF, wide), 1) + part * HALF
            here = lax.broadcasted_iota(jnp.int32, (HALF, wide), 0) + (part * HALF + SPAN)
            low = low_ref[part * HALF : (part + 1) * HALF, :] + SPAN
            keep = (key >= low) & (key <= here)
            bias[part] = jnp.where(keep, 0.0, -1e30)

    for h in range(PER_STEP):
        lanes = slice(h * HEAD, (h + 1) * HEAD)
        q = q_ref[:, :, lanes].reshape(SPAN, HEAD)
        k = jnp.concatenate([before_ref[:, 0, :, lanes].reshape(SPAN, HEAD), own_ref[:, 0, :, lanes].reshape(SPAN, HEAD)], 0)
        v = jnp.concatenate([before_ref[:, 1, :, lanes].reshape(SPAN, HEAD), own_ref[:, 1, :, lanes].reshape(SPAN, HEAD)], 0)
        for part in range(2):
            rows = slice(part * HALF, (part + 1) * HALF)
            keys = slice(part * HALF, part * HALF + wide)
            scores = dot(q[rows], k[keys], NT) + bias[part]
            top = jnp.max(scores, axis=1, keepdims=True)
            raised = jnp.exp2((scores - top) * factor)
            total = jnp.sum(raised, axis=1, keepdims=True)
            context = dot(raised.astype(jnp.bfloat16), v[keys]) / total
            out_ref[rows, lanes] = context.astype(jnp.bfloat16)
    turn = HALF - 1 - lax.broadcasted_iota(jnp.int32, (HALF, 1), 0)
    context = out_ref[...]
    ahead_ref[...] = dot(one_hot(edge_ref[0] + turn, HALF, SPAN), context).astype(jnp.bfloat16)
    back_ref[...] = dot(one_hot(edge_ref[1] - HALF + turn, HALF, SPAN), context).astype(jnp.bfloat16)


def attend(edge, low, q, own, before):
    features = q.shape[2]
    lanes = PER_STEP * HEAD
    pieces, piece = q.shape[0], q.shape[1]
    pair = pl.BlockSpec((pieces, 2, piece, lanes), lambda g: (0, 0, 0, g))
    return pl.pallas_call(
        attend_kernel,
        grid=(features // lanes,),
        in_specs=[
            pl.BlockSpec(memory_space=pltpu.SMEM),
            pl.BlockSpec((SPAN, 1), lambda g: (0, 0)),
            pl.BlockSpec((pieces, piece, lanes), lambda g: (0, 0, g)),
            pair,
            pair,
        ],
        out_specs=[
            pl.BlockSpec((SPAN, lanes), lambda g: (0, g)),
            pl.BlockSpec((HALF, lanes), lambda g: (0, g)),
            pl.BlockSpec((HALF, lanes), lambda g: (0, g)),
        ],
        out_shape=[
            jax.ShapeDtypeStruct((SPAN, features), jnp.bfloat16),
            jax.ShapeDtypeStruct((HALF, features), jnp.bfloat16),
            jax.ShapeDtypeStruct((HALF, features), jnp.bfloat16),
        ],
        scratch_shapes=[pltpu.VMEM((2, HALF, SPAN + HALF), jnp.float32)],
        compiler_params=pltpu.CompilerParams(vmem_limit_bytes=32 * 2**20),
        cost_estimate=pl.CostEstimate(flops=10**9, bytes_accessed=4 * 2**20, transcendentals=10**6),
        name="attend",
    )(edge, low, q, own, before)


def mirror_kernel(source_ref, own_ref, before_ref, after_ref, out_ref):
    source = source_ref[...]
    out = dot(one_hot(source, SPAN, SPAN), own_ref[...])
    out = out + dot(one_hot(source - SPAN, SPAN, HALF), before_ref[...])
    out = out + dot(one_hot(source - SPAN - HALF, SPAN, HALF), after_ref[...])
    out_ref[...] = out.astype(jnp.bfloat16)


def mirrored(source, own, before, after):
    return pl.pallas_call(
        mirror_kernel,
        out_shape=jax.ShapeDtypeStruct(own.shape, jnp.bfloat16),
        compiler_params=pltpu.CompilerParams(vmem_limit_bytes=32 * 2**20),
        cost_estimate=pl.CostEstimate(flops=3 * 10**8, bytes_accessed=2 * 2**20, transcendentals=0),
        name="mirror",
    )(source, own, before, after)


def join_kernel(side_ref, mine_ref, other_ref, weight_ref, second_ref, out_ref):
    depth = mine_ref.shape[1]
    wide = out_ref.shape[2]
    total = dot(mine_ref[...], weight_ref[...].reshape(depth, wide))
    total = total + dot(other_ref[...], second_ref[...].reshape(depth, wide))
    out_ref[...] = total.astype(jnp.bfloat16).reshape(out_ref.shape)


def join(side, mine, other, weight, pieces):
    tokens, depth = mine.shape
    heads, _, head, units = weight.shape
    wide = 256
    whole = pl.BlockSpec((tokens, depth), lambda n, side: (0, 0))
    return pl.pallas_call(
        join_kernel,
        grid_spec=pltpu.PrefetchScalarGridSpec(
            num_scalar_prefetch=1,
            grid=(units // wide,),
            in_specs=[
                whole,
                whole,
                pl.BlockSpec((heads, 1, head, wide), lambda n, side: (0, side[0], 0, n)),
                pl.BlockSpec((heads, 1, head, wide), lambda n, side: (0, 1 - side[0], 0, n)),
            ],
            out_specs=pl.BlockSpec((pieces, tokens // pieces, wide), lambda n, side: (0, 0, n)),
        ),
        out_shape=jax.ShapeDtypeStruct((pieces, tokens // pieces, units), jnp.bfloat16),
        compiler_params=pltpu.CompilerParams(vmem_limit_bytes=32 * 2**20),
        cost_estimate=pl.CostEstimate(flops=10**9, bytes_accessed=6 * 2**20, transcendentals=0),
        name="join",
    )(side, mine, other, weight, weight)


def body(queries, key_states, value_vectors, hypothesis_lengths, join_weight):
    _, rows, piece, width = queries.shape
    pieces = SPAN // piece
    share = width // pieces
    side = lax.axis_index("dir")
    ring = lax.axis_index("y") * 8 + lax.axis_index("z")
    base = ring * SPAN

    def exchange(parts):
        return lax.all_to_all(parts, "x", split_axis=0, concat_axis=0, tiled=True)

    def split(states):
        return states.reshape(piece, pieces, share).transpose(1, 0, 2)

    turned = lax.ppermute(
        join_weight.reshape(piece, -1), ("y", "x"), [(y * 4 + x, x * 4 + y) for y in range(4) for x in range(4)]
    )
    weight = lax.all_gather(turned, ("z", "y"), tiled=True)
    units = weight.shape[1]
    weight = weight.reshape(share // HEAD, 2, HEAD, units)

    first, end = tables(hypothesis_lengths, base)
    here = jnp.arange(SPAN, dtype=jnp.int32)[None, :]
    mirror = first + end - 1 - here
    source = jnp.where(
        mirror < 0, SPAN + here - end + HALF, jnp.where(mirror >= SPAN, SPAN + HALF + here - first, mirror)
    )
    source = jnp.where(side == 0, here, source)
    edges = jnp.stack([first[:, -1], end[:, 0]], axis=1)

    next_ring = [(c, c + 1) for c in range(RINGS - 1)]
    swap_ahead = [(RINGS + c, RINGS + c + 1) for c in range(RINGS - 1)]
    swap_back = [(RINGS + c + 1, RINGS + c) for c in range(RINGS - 1)]
    joined = []
    for r in range(rows):
        own = exchange(jnp.stack([split(key_states[0, r]), split(value_vectors[0, r])], axis=1))
        q = exchange(split(queries[0, r]))
        before = lax.ppermute(own, ("y", "z"), next_ring)
        context, ahead, back = attend(edges[r], first[r][:, None], q, own, before)
        from_before = lax.ppermute(ahead, ("dir", "y", "z"), swap_ahead)
        from_after = lax.ppermute(back, ("dir", "y", "z"), swap_back)
        mine = mirrored(source[r][:, None], context, from_before, from_after)
        other = lax.ppermute(mine, "dir", [(0, 1), (1, 0)])
        partial_value = join(side[None], mine, other, weight, pieces)
        total = jnp.sum(exchange(partial_value).astype(jnp.float32), axis=0)
        joined.append((jax.nn.silu(total[:, : units // 2]) * total[:, units // 2 :]).astype(jnp.bfloat16))
    return jnp.stack(joined)


def solution(mesh):
    fine = Mesh(mesh.devices.reshape(2, 4, 8, 4), ("dir", "y", "z", "x"))
    states = P("dir", None, ("y", "z", "x"), None)
    return jax.shard_map(
        body,
        mesh=fine,
        in_specs=(states, states, states, P(), P(("y", "z", "x"), None, "dir")),
        out_specs=P(None, ("y", "z", "x"), "dir"),
        check_vma=False,
    )
```

```python
import math

import jax
import jax.numpy as jnp
from jax import lax
from jax.experimental import pallas as pl
from jax.experimental.pallas import tpu as pltpu
from jax.sharding import Mesh
from jax.sharding import PartitionSpec as P

HEAD = 128
SPAN = 256
HALF = SPAN // 2
RINGS = 32
PER_STEP = 2
CHUNKS = ((0, 1), (1, 3), (3, 4))
NT = (((1,), (1,)), ((), ()))
NN = (((1,), (0,)), ((), ()))
ANYWHERE = pl.BlockSpec(memory_space=pl.ANY)
PARAMS = pltpu.CompilerParams(vmem_limit_bytes=32 * 2**20)


def dot(a, b, dims=NN):
    return lax.dot_general(a, b, dims, preferred_element_type=jnp.float32)


def one_hot(index, rows, columns):
    at = lax.broadcasted_iota(jnp.int32, (rows, columns), 1)
    return jnp.where(at == index, 1.0, 0.0).astype(jnp.bfloat16)


def cost(flops, nbytes):
    return pl.CostEstimate(flops=flops, bytes_accessed=nbytes, transcendentals=0)


def table_kernel(place_ref, lengths_ref, first_ref, end_ref, source_ref):
    rows, count = lengths_ref.shape
    base, side = place_ref[0], place_ref[1]
    lengths = lengths_ref[...].astype(jnp.float32)
    upto = lax.broadcasted_iota(jnp.int32, (count, count), 0) <= lax.broadcasted_iota(jnp.int32, (count, count), 1)
    ends = dot(lengths.astype(jnp.bfloat16), jnp.where(upto, 1.0, 0.0).astype(jnp.bfloat16))
    starts = ends - lengths
    here = lax.broadcasted_iota(jnp.int32, (SPAN, 1), 0)
    at = (here + base).astype(jnp.float32)
    for r in range(rows):
        start, stop = starts[r : r + 1], ends[r : r + 1]
        first = jnp.max(jnp.where(start <= at, start, 0.0), axis=1, keepdims=True).astype(jnp.int32) - base
        end = jnp.min(jnp.where(stop > at, stop, 1e9), axis=1, keepdims=True).astype(jnp.int32) - base
        mirror = first + end - 1 - here
        source = jnp.where(
            mirror < 0, SPAN + here - end + HALF, jnp.where(mirror >= SPAN, SPAN + HALF + here - first, mirror)
        )
        first_ref[r] = first
        end_ref[r] = end
        source_ref[r] = jnp.where(side == 0, here, source)


def tables(place, lengths):
    column = jax.ShapeDtypeStruct((lengths.shape[0], SPAN, 1), jnp.int32)
    return pl.pallas_call(
        table_kernel,
        in_specs=[pl.BlockSpec(memory_space=pltpu.SMEM), pl.BlockSpec(memory_space=pltpu.VMEM)],
        out_shape=[column] * 3,
        compiler_params=PARAMS,
        cost_estimate=cost(1, 1),
        name="tables",
    )(place, lengths)


def pack_kernel(count, *refs):
    out_ref = refs[-1]
    pieces, share = out_ref.shape[0], out_ref.shape[-1]
    for t in range(count):
        for f in range(pieces):
            out_ref[f, 0, t] = refs[t][0, 0, :, f * share : (f + 1) * share]


def pack(states, chunk, pieces, after=()):
    low, high = chunk
    _, _, piece, width = states[0].shape
    share = width // pieces
    count = len(states)
    shape = (pieces, high - low, count, piece, share)
    return pl.pallas_call(
        lambda *refs: pack_kernel(count, *refs),
        grid=(high - low,),
        in_specs=[pl.BlockSpec((1, 1, piece, width), lambda r: (0, r + low, 0, 0))] * count + [ANYWHERE] * len(after),
        out_specs=pl.BlockSpec((pieces, 1, count, piece, share), lambda r: (0, r, 0, 0, 0)),
        out_shape=jax.ShapeDtypeStruct(shape, jnp.bfloat16),
        compiler_params=PARAMS,
        cost_estimate=cost(1, 1),
        name="pack",
    )(*states, *after)


def attend_kernel(first_ref, end_ref, q_ref, own_ref, before_ref, *refs):
    out_ref, ahead_ref, back_ref, bias = refs[-4:]
    factor = math.log2(math.e) / math.sqrt(HEAD)
    wide = SPAN + HALF

    @pl.when(pl.program_id(1) == 0)
    def _():
        for part in range(2):
            key = lax.broadcasted_iota(jnp.int32, (HALF, wide), 1) + part * HALF
            here = lax.broadcasted_iota(jnp.int32, (HALF, wide), 0) + (part * HALF + SPAN)
            low = first_ref[0, part * HALF : (part + 1) * HALF, :] + SPAN
            keep = (key >= low) & (key <= here)
            bias[part] = jnp.where(keep, 0.0, -1e30)

    def keyed(index, lanes):
        return jnp.concatenate(
            [before_ref[:, 0, index, :, lanes].reshape(SPAN, HEAD), own_ref[:, 0, index, :, lanes].reshape(SPAN, HEAD)], 0
        )

    for h in range(PER_STEP):
        lanes = slice(h * HEAD, (h + 1) * HEAD)
        q = q_ref[:, 0, 0, :, lanes].reshape(SPAN, HEAD)
        k, v = keyed(0, lanes), keyed(1, lanes)
        for part in range(2):
            rows = slice(part * HALF, (part + 1) * HALF)
            keys = slice(part * HALF, part * HALF + wide)
            scores = dot(q[rows], k[keys], NT) + bias[part]
            top = jnp.max(scores, axis=1, keepdims=True)
            raised = jnp.exp2((scores - top) * factor)
            total = jnp.sum(raised, axis=1, keepdims=True)
            context = dot(raised.astype(jnp.bfloat16), v[keys]) / total
            out_ref[0, rows, lanes] = context.astype(jnp.bfloat16)
    turn = HALF - 1 - lax.broadcasted_iota(jnp.int32, (HALF, 1), 0)
    context = out_ref[0]
    ahead = first_ref[0, SPAN - 1 :, :] + turn
    ahead_ref[0] = dot(one_hot(ahead, HALF, SPAN), context).astype(jnp.bfloat16)
    back = end_ref[0, :1, :] - HALF + turn
    back_ref[0] = dot(one_hot(back, HALF, SPAN), context).astype(jnp.bfloat16)


def attend(first, end, q, own, before, low, after=()):
    pieces, rows, _, piece, features = own.shape
    lanes = PER_STEP * HEAD
    column = pl.BlockSpec((1, SPAN, 1), lambda r, g: (r + low, 0, 0))
    pair = pl.BlockSpec((pieces, 1, 2, piece, lanes), lambda r, g: (0, r, 0, 0, g))

    def out(tokens):
        return pl.BlockSpec((1, tokens, lanes), lambda r, g: (r, 0, g))

    return pl.pallas_call(
        attend_kernel,
        grid=(rows, features // lanes),
        in_specs=[
            column,
            column,
            pl.BlockSpec((pieces, 1, 1, piece, lanes), lambda r, g: (0, r + low, 0, 0, g)),
            pair,
            pair,
            *[ANYWHERE] * len(after),
        ],
        out_specs=[out(SPAN), out(HALF), out(HALF)],
        out_shape=[jax.ShapeDtypeStruct((rows, tokens, features), jnp.bfloat16) for tokens in (SPAN, HALF, HALF)],
        scratch_shapes=[pltpu.VMEM((2, HALF, SPAN + HALF), jnp.float32)],
        compiler_params=PARAMS,
        cost_estimate=cost(rows * 10**10, rows * 4 * 2**20),
        name="attend",
    )(first, end, q, own, before, *after)


def mirror_kernel(source_ref, own_ref, before_ref, after_ref, out_ref):
    source = source_ref[0]
    out = dot(one_hot(source, SPAN, SPAN), own_ref[0])
    out = out + dot(one_hot(source - SPAN, SPAN, HALF), before_ref[0])
    out = out + dot(one_hot(source - SPAN - HALF, SPAN, HALF), after_ref[0])
    out_ref[0] = out.astype(jnp.bfloat16)


def mirrored(source, own, before, after, low):
    rows, _, features = own.shape

    def block(tokens):
        return pl.BlockSpec((1, tokens, features), lambda r: (r, 0, 0))

    return pl.pallas_call(
        mirror_kernel,
        grid=(rows,),
        in_specs=[pl.BlockSpec((1, SPAN, 1), lambda r: (r + low, 0, 0)), block(SPAN), block(HALF), block(HALF)],
        out_specs=block(SPAN),
        out_shape=jax.ShapeDtypeStruct(own.shape, jnp.bfloat16),
        compiler_params=PARAMS,
        cost_estimate=cost(1, 1),
        name="mirror",
    )(source, own, before, after)


def join_kernel(side_ref, mine_ref, other_ref, weight_ref, second_ref, *refs):
    out_ref = refs[-1]
    rows, tokens, depth = mine_ref.shape
    pieces, _, piece, wide = out_ref.shape
    weight = weight_ref[...].reshape(depth, wide)
    second = second_ref[...].reshape(depth, wide)
    for r in range(rows):
        total = dot(mine_ref[r], weight) + dot(other_ref[r], second)
        out_ref[:, r] = total.astype(jnp.bfloat16).reshape(pieces, piece, wide)


def join(side, mine, other, weight, pieces, after=()):
    rows, tokens, depth = mine.shape
    heads, _, head, units = weight.shape
    wide = units // 2
    whole = pl.BlockSpec((rows, tokens, depth), lambda n, side: (0, 0, 0))
    return pl.pallas_call(
        join_kernel,
        grid_spec=pltpu.PrefetchScalarGridSpec(
            num_scalar_prefetch=1,
            grid=(units // wide,),
            in_specs=[
                whole,
                whole,
                pl.BlockSpec((heads, 1, head, wide), lambda n, side: (0, side[0], 0, n)),
                pl.BlockSpec((heads, 1, head, wide), lambda n, side: (0, 1 - side[0], 0, n)),
                *[ANYWHERE] * len(after),
            ],
            out_specs=pl.BlockSpec((pieces, rows, tokens // pieces, wide), lambda n, side: (0, 0, 0, n)),
        ),
        out_shape=jax.ShapeDtypeStruct((pieces, rows, tokens // pieces, units), jnp.bfloat16),
        compiler_params=PARAMS,
        cost_estimate=cost(1, 1),
        name="join",
    )(side, mine, other, weight, weight, *after)


def body(queries, key_states, value_vectors, hypothesis_lengths, join_weight):
    _, rows, piece, width = queries.shape
    pieces = SPAN // piece
    share = width // pieces
    side = lax.axis_index("dir")
    ring = lax.axis_index("y") * 8 + lax.axis_index("z")

    def exchange(parts):
        return lax.all_to_all(parts, "x", split_axis=0, concat_axis=0, tiled=True)

    next_ring = [(c, c + 1) for c in range(RINGS - 1)]
    swap_ahead = [(RINGS + c, RINGS + c + 1) for c in range(RINGS - 1)]
    swap_back = [(RINGS + c + 1, RINGS + c) for c in range(RINGS - 1)]

    def forward(own):
        return lax.ppermute(own, ("y", "z"), next_ring)

    turned = lax.ppermute(
        join_weight.reshape(piece, -1), ("y", "x"), [(y * 4 + x, x * 4 + y) for y in range(4) for x in range(4)]
    )
    weight = lax.all_gather(turned, ("z", "y"), tiled=True)
    units = weight.shape[1]
    weight = weight.reshape(share // HEAD, 2, HEAD, units)
    first, end, source = tables(jnp.stack([ring * SPAN, side]).astype(jnp.int32), hypothesis_lengths)

    both = (key_states, value_vectors)
    own, before = [None] * 3, [None] * 3
    own[0] = exchange(pack(both, CHUNKS[0], pieces))
    before[0] = forward(own[0])
    own[1] = exchange(pack(both, CHUNKS[1], pieces, (own[0],)))
    before[1] = forward(own[1])
    q = exchange(pack((queries,), (0, rows), pieces, (own[1], before[0])))

    def contexts(i, after):
        return attend(first, end, q, own[i], before[i], CHUNKS[i][0], after)

    def swapped(i, parts):
        context, ahead, back = parts
        from_before = lax.ppermute(ahead, ("dir", "y", "z"), swap_ahead)
        from_after = lax.ppermute(back, ("dir", "y", "z"), swap_back)
        mine = mirrored(source, context, from_before, from_after, CHUNKS[i][0])
        return mine, lax.ppermute(mine, "dir", [(0, 1), (1, 0)])

    def gated(partial_value):
        total = jnp.sum(exchange(partial_value).astype(jnp.float32), axis=0)
        return (jax.nn.silu(total[..., : units // 2]) * total[..., units // 2 :]).astype(jnp.bfloat16)

    parts = [contexts(0, ())]
    own[2] = exchange(pack(both, CHUNKS[2], pieces, (q, parts[0][1])))
    before[2] = forward(own[2])
    parts.append(contexts(1, (own[2],)))
    partials = [join(side[None], *swapped(0, parts[0]), weight, pieces)]
    parts.append(contexts(2, (parts[1][1], partials[0])))
    partials.append(join(side[None], *swapped(1, parts[1]), weight, pieces))
    partials.append(join(side[None], *swapped(2, parts[2]), weight, pieces, (partials[1],)))
    joined = [gated(partial_value) for partial_value in partials]
    return jnp.concatenate(joined)


def solution(mesh):
    fine = Mesh(mesh.devices.reshape(2, 4, 8, 4), ("dir", "y", "z", "x"))
    states = P("dir", None, ("y", "z", "x"), None)
    return jax.shard_map(
        body,
        mesh=fine,
        in_specs=(states, states, states, P(), P(("y", "z", "x"), None, "dir")),
        out_specs=P(None, ("y", "z", "x"), "dir"),
        check_vma=False,
    )
```

```python
import math

import jax
import jax.numpy as jnp
from jax import lax
from jax.experimental import pallas as pl
from jax.experimental.pallas import tpu as pltpu
from jax.sharding import Mesh
from jax.sharding import PartitionSpec as P

HEAD = 128
SPAN = 256
HALF = SPAN // 2
RINGS = 32
LONG = 10**10
CHUNKS = ((0, 1), (1, 3), (3, 4))
NT = (((1,), (1,)), ((), ()))
NN = (((1,), (0,)), ((), ()))
TN = (((0,), (0,)), ((), ()))
PARAMS = pltpu.CompilerParams(vmem_limit_bytes=16 * 2**20)


def dot(a, b, dims=NN):
    return lax.dot_general(a, b, dims, preferred_element_type=jnp.float32)


def cost(flops, nbytes):
    return pl.CostEstimate(flops=flops, bytes_accessed=nbytes, transcendentals=0)


def table_kernel(place_ref, lengths_ref, first_ref, here_ref, ahead_ref):
    rows, count = lengths_ref.shape
    base, side = place_ref[0], place_ref[1]
    lengths = lengths_ref[...].astype(jnp.float32)
    upto = lax.broadcasted_iota(jnp.int32, (count, count), 1) <= lax.broadcasted_iota(jnp.int32, (count, count), 0)
    before = lax.broadcasted_iota(jnp.int32, (count, count), 1) < lax.broadcasted_iota(jnp.int32, (count, count), 0)
    lengths = lengths.astype(jnp.bfloat16)
    ends = dot(jnp.where(upto, 1.0, 0.0).astype(jnp.bfloat16), lengths, NT)
    starts = dot(jnp.where(before, 1.0, 0.0).astype(jnp.bfloat16), lengths, NT)
    place = lax.broadcasted_iota(jnp.int32, (1, 2 * SPAN), 1)
    at = (place + base).astype(jnp.float32)
    for r in range(rows):
        start, stop = starts[:, r : r + 1], ends[:, r : r + 1]
        first = jnp.max(jnp.where(start <= at, start, 0.0), axis=0, keepdims=True).astype(jnp.int32) - base
        end = jnp.min(jnp.where(stop > at, stop, 1e6), axis=0, keepdims=True).astype(jnp.int32) - base
        mirror = jnp.where((first >= 0) & (first < SPAN), first + end - 1 - place, -1)
        first_ref[r] = first
        here_ref[r] = jnp.where(side == 0, place[:, SPAN:], mirror[:, :SPAN])
        ahead_ref[r] = mirror[:, SPAN:]


def tables(place, lengths):
    rows = lengths.shape[0]
    return pl.pallas_call(
        table_kernel,
        in_specs=[pl.BlockSpec(memory_space=pltpu.SMEM), pl.BlockSpec(memory_space=pltpu.VMEM)],
        out_shape=[jax.ShapeDtypeStruct((rows, 1, n), jnp.int32) for n in (2 * SPAN, SPAN, SPAN)],
        compiler_params=PARAMS,
        cost_estimate=cost(1, 1),
        name="tables",
    )(place, lengths)


def pack_kernel(count, low, *refs):
    out_ref, done = refs[-2:]
    pieces, rows, _, _, share = out_ref.shape
    copies = []
    for r in range(rows):
        for t in range(count):
            for f in range(pieces):
                part = refs[t].at[0, low + r, :, pl.ds(f * share, share)]
                copies.append(pltpu.make_async_copy(part, out_ref.at[f, r, t], done.at[len(copies)]))
    for copy in copies:
        copy.start()
    for copy in copies:
        copy.wait()


def first_tile(array):
    lead = len(array.shape) - 2
    return pl.BlockSpec((1,) * lead + (16, 128), lambda *_: (0,) * (lead + 2))


def pack(states, chunk, pieces, after=(), weight=1):
    low, high = chunk
    _, _, piece, width = states[0].shape
    share = width // pieces
    count = len(states)
    shape = (pieces, high - low, count, piece, share)
    return pl.pallas_call(
        lambda *refs: pack_kernel(count, low, *refs),
        grid=(1,),
        in_specs=[pl.BlockSpec(memory_space=pltpu.HBM)] * count + [first_tile(array) for array in after],
        out_specs=pl.BlockSpec(memory_space=pltpu.HBM),
        out_shape=pltpu.HBM(shape, jnp.bfloat16),
        scratch_shapes=[pltpu.SemaphoreType.DMA((pieces * (high - low) * count,))],
        compiler_params=PARAMS,
        cost_estimate=cost(weight, 1),
        name="pack",
    )(*[pltpu.with_memory_space_constraint(state, pltpu.HBM) for state in states], *after)


def attend_kernel(
    side_ref, first_ref, here_ref, ahead_ref, q_ref, next_q_ref, own_ref, other_ref, *refs
):
    out_ref, sent_ref, keys, values, later, contexts = refs[-6:]
    factor = math.log2(math.e) / math.sqrt(HEAD)
    features = keys.shape[1]
    low, high = slice(0, SPAN), slice(SPAN, 2 * SPAN)

    def flat(ref, index):
        return ref[:, 0, index].reshape(SPAN, features)

    @pl.when(side_ref[0] == 0)
    def _():
        keys[low], keys[high] = flat(other_ref, 0), flat(own_ref, 0)
        values[low], values[high] = flat(other_ref, 1), flat(own_ref, 1)
        later[...] = flat(q_ref, 0)

    @pl.when(side_ref[0] != 0)
    def _():
        keys[low], keys[high] = flat(own_ref, 0), flat(other_ref, 0)
        values[low], values[high] = flat(own_ref, 1), flat(other_ref, 1)
        later[...] = flat(next_q_ref, 0)

    blocks = []
    for block in range(4):
        spot = block * HALF
        at = slice(max(0, spot - SPAN), spot + HALF)
        wide = at.stop - at.start
        key = lax.broadcasted_iota(jnp.int32, (wide, HALF), 0) + at.start
        here = lax.broadcasted_iota(jnp.int32, (wide, HALF), 1) + spot
        keep = (key >= first_ref[0, :, spot : spot + HALF]) & (key <= here)
        blocks.append((spot, at, jnp.where(keep, 0.0, -1e30)))
    for spot, at, bias in blocks:
        for h in range(features // HEAD):
            lanes = slice(h * HEAD, (h + 1) * HEAD)
            if spot < SPAN:
                piece = q_ref.shape[3]
                some = slice(spot // piece, (spot + HALF) // piece)
                q = q_ref[some, 0, 0, :, lanes].reshape(HALF, HEAD)
            else:
                q = later[spot - SPAN : spot - SPAN + HALF, lanes]
            scores = dot(keys[at, lanes], q, NT) + bias
            top = jnp.max(scores, axis=0, keepdims=True)
            raised = jnp.exp2((scores - top) * factor)
            total = jnp.sum(raised, axis=0, keepdims=True)
            weights = (raised * (1.0 / total)).astype(jnp.bfloat16)
            contexts[spot : spot + HALF, lanes] = dot(weights, values[at, lanes], TN).astype(jnp.bfloat16)
    source = lax.broadcasted_iota(jnp.int32, (2 * SPAN, SPAN), 0)
    for index, ref in ((here_ref[0], out_ref), (ahead_ref[0], sent_ref)):
        chosen = jnp.where(source == index, 1.0, 0.0).astype(jnp.bfloat16)
        ref[0] = dot(chosen, contexts[...], TN).astype(jnp.bfloat16)


def attend(side, first, here, ahead, q, next_q, own, other, low, low_q, after, weight):
    pieces, rows, _, piece, features = own.shape

    def line(array):
        return pl.BlockSpec((1, 1, array.shape[2]), lambda r: (r + low, 0, 0))

    def states(array, at):
        return pl.BlockSpec((pieces, 1, array.shape[2], piece, features), lambda r: (0, r + at, 0, 0, 0))

    block = pl.BlockSpec((1, SPAN, features), lambda r: (r, 0, 0))
    return pl.pallas_call(
        attend_kernel,
        grid=(rows,),
        in_specs=[
            pl.BlockSpec(memory_space=pltpu.SMEM),
            line(first),
            line(here),
            line(ahead),
            states(q, low_q),
            states(next_q, low_q),
            states(own, 0),
            states(other, 0),
            *[first_tile(array) for array in after],
        ],
        out_specs=[block, block],
        out_shape=[jax.ShapeDtypeStruct((rows, SPAN, features), jnp.bfloat16)] * 2,
        scratch_shapes=[
            pltpu.VMEM((2 * SPAN, features), jnp.bfloat16),
            pltpu.VMEM((2 * SPAN, features), jnp.bfloat16),
            pltpu.VMEM((SPAN, features), jnp.bfloat16),
            pltpu.VMEM((2 * SPAN, features), jnp.bfloat16),
        ],
        compiler_params=pltpu.CompilerParams(vmem_limit_bytes=28 * 2**20),
        cost_estimate=cost(rows * weight, 1),
        name="attend",
    )(side, first, here, ahead, q, next_q, own, other, *after)


def join_kernel(side_ref, mine_ref, other_ref, weight_ref, second_ref, *refs):
    out_ref = refs[-1]
    rows, tokens, depth = mine_ref.shape
    pieces, _, piece, wide = out_ref.shape
    weight = weight_ref[...].reshape(depth, wide)
    second = second_ref[...].reshape(depth, wide)
    for r in range(rows):
        total = dot(mine_ref[r], weight) + dot(other_ref[r], second)
        out_ref[:, r] = total.astype(jnp.bfloat16).reshape(pieces, piece, wide)


def join(side, mine, other, weight, pieces, after=()):
    rows, tokens, depth = mine.shape
    heads, _, head, units = weight.shape
    wide = units // 2
    whole = pl.BlockSpec((rows, tokens, depth), lambda n, side: (0, 0, 0))
    return pl.pallas_call(
        join_kernel,
        grid_spec=pltpu.PrefetchScalarGridSpec(
            num_scalar_prefetch=1,
            grid=(units // wide,),
            in_specs=[
                whole,
                whole,
                pl.BlockSpec((heads, 1, head, wide), lambda n, side: (0, side[0], 0, n)),
                pl.BlockSpec((heads, 1, head, wide), lambda n, side: (0, 1 - side[0], 0, n)),
                *[first_tile(array) for array in after],
            ],
            out_specs=pl.BlockSpec((pieces, rows, tokens // pieces, wide), lambda n, side: (0, 0, 0, n)),
        ),
        out_shape=jax.ShapeDtypeStruct((pieces, rows, tokens // pieces, units), jnp.bfloat16),
        compiler_params=PARAMS,
        cost_estimate=cost(1, 1),
        name="join",
    )(side, mine, other, weight, weight, *after)


def body(queries, key_states, value_vectors, hypothesis_lengths, join_weight):
    _, rows, piece, width = queries.shape
    pieces = SPAN // piece
    share = width // pieces
    side = lax.axis_index("dir")
    ring = lax.axis_index("y") * 8 + lax.axis_index("z")

    def exchange(parts):
        return lax.all_to_all(parts, "x", split_axis=0, concat_axis=0, tiled=True)

    to_left = [(RINGS + c + 1, RINGS + c) for c in range(RINGS - 1)]
    to_right = [(RINGS + c, RINGS + c + 1) for c in range(RINGS - 1)]
    outward = [(c, c + 1) for c in range(RINGS - 1)] + to_left

    def passed(array, pairs):
        return lax.ppermute(array, ("dir", "y", "z"), pairs)

    turned = lax.ppermute(
        join_weight.reshape(piece, -1), ("y", "x"), [(y * 4 + x, x * 4 + y) for y in range(4) for x in range(4)]
    )
    weight = lax.all_gather(turned, ("z", "y"), tiled=True)
    units = weight.shape[1]
    weight_rows = weight.reshape(share // HEAD, 2, HEAD, units)
    base = (ring - 1 + side) * SPAN
    lines = tables(jnp.stack([base, side]).astype(jnp.int32), hypothesis_lengths)

    both = (key_states, value_vectors)
    own, other = [None] * 3, [None] * 3
    own[0] = exchange(pack(both, CHUNKS[0], pieces))
    other[0] = passed(own[0], outward)
    q_most = exchange(pack((queries,), (0, 3), pieces, (own[0], turned)))
    next_most = passed(q_most, to_left)
    own[1] = exchange(pack(both, CHUNKS[1], pieces, (q_most, other[0])))
    other[1] = passed(own[1], outward)
    own[2] = exchange(pack(both, CHUNKS[2], pieces, (own[1], next_most)))
    other[2] = passed(own[2], outward)

    def contexts(i, q, next_q, low_q, after=(), weight=LONG):
        low = CHUNKS[i][0]
        return attend(side[None], *lines, q, next_q, own[i], other[i], low, low_q, after, weight)

    def swapped(mine, ahead):
        mine = mine + passed(ahead, to_right)
        return mine, lax.ppermute(mine, "dir", [(0, 1), (1, 0)])

    def joined_part(mine, partner, after=()):
        return join(side[None], mine, partner, weight_rows, pieces, after)

    def gated(arrived):
        total = jnp.sum(arrived.astype(jnp.float32), axis=0)
        return (jax.nn.silu(total[..., : units // 2]) * total[..., units // 2 :]).astype(jnp.bfloat16)

    first_part = contexts(0, q_most, next_most, CHUNKS[0][0])
    q_last = exchange(pack((queries,), (3, 4), pieces, (own[2], first_part[1])))
    next_last = passed(q_last, to_left)
    first_part = swapped(*first_part)
    second_part = contexts(1, q_most, next_most, CHUNKS[1][0], (q_last, first_part[0]))
    third_part = contexts(2, q_last, next_last, 0, (second_part[1], first_part[1]))
    arrived = [exchange(joined_part(*first_part))]
    partial_value = joined_part(*swapped(*second_part), ())
    arrived.append(exchange(partial_value))
    arrived.append(exchange(joined_part(*swapped(*third_part), (arrived[0], partial_value))))
    joined = [gated(one) for one in arrived]
    return jnp.concatenate(joined)


def solution(mesh):
    fine = Mesh(mesh.devices.reshape(2, 4, 8, 4), ("dir", "y", "z", "x"))
    states = P("dir", None, ("y", "z", "x"), None)
    return jax.shard_map(
        body,
        mesh=fine,
        in_specs=(states, states, states, P(), P(("y", "z", "x"), None, "dir")),
        out_specs=P(None, ("y", "z", "x"), "dir"),
        check_vma=False,
    )
```

```python
import math

import jax
import jax.numpy as jnp
from jax import lax
from jax.experimental import pallas as pl
from jax.experimental.pallas import tpu as pltpu
from jax.sharding import Mesh
from jax.sharding import PartitionSpec as P

HEAD = 128
SPAN = 256
HALF = SPAN // 2
RINGS = 32
LONG = 10**10
CHUNKS = ((0, 2), (2, 4))
NT = (((1,), (1,)), ((), ()))
NN = (((1,), (0,)), ((), ()))
TN = (((0,), (0,)), ((), ()))
PARAMS = pltpu.CompilerParams(vmem_limit_bytes=16 * 2**20)


def dot(a, b, dims=NN):
    return lax.dot_general(a, b, dims, preferred_element_type=jnp.float32)


def cost(flops, nbytes):
    return pl.CostEstimate(flops=flops, bytes_accessed=nbytes, transcendentals=0)


def table_kernel(place_ref, lengths_ref, first_ref, here_ref, ahead_ref):
    rows, count = lengths_ref.shape
    base = place_ref[0]
    lengths = lengths_ref[...].astype(jnp.float32)
    upto = lax.broadcasted_iota(jnp.int32, (count, count), 1) <= lax.broadcasted_iota(jnp.int32, (count, count), 0)
    before = lax.broadcasted_iota(jnp.int32, (count, count), 1) < lax.broadcasted_iota(jnp.int32, (count, count), 0)
    lengths = lengths.astype(jnp.bfloat16)
    ends = dot(jnp.where(upto, 1.0, 0.0).astype(jnp.bfloat16), lengths, NT)
    starts = dot(jnp.where(before, 1.0, 0.0).astype(jnp.bfloat16), lengths, NT)
    place = lax.broadcasted_iota(jnp.int32, (1, 2 * SPAN), 1)
    at = (place + base).astype(jnp.float32)
    for r in range(rows):
        start, stop = starts[:, r : r + 1], ends[:, r : r + 1]
        first = jnp.max(jnp.where(start <= at, start, 0.0), axis=0, keepdims=True).astype(jnp.int32) - base
        end = jnp.min(jnp.where(stop > at, stop, 1e6), axis=0, keepdims=True).astype(jnp.int32) - base
        mirror = jnp.where((first >= 0) & (first < SPAN), first + end - 1 - place, -1)
        first_ref[r] = first
        here_ref[r] = mirror[:, :SPAN]
        ahead_ref[r] = mirror[:, SPAN:]


def tables(place, lengths):
    rows = lengths.shape[0]
    return pl.pallas_call(
        table_kernel,
        in_specs=[pl.BlockSpec(memory_space=pltpu.SMEM), pl.BlockSpec(memory_space=pltpu.VMEM)],
        out_shape=[jax.ShapeDtypeStruct((rows, 1, n), jnp.int32) for n in (2 * SPAN, SPAN, SPAN)],
        compiler_params=PARAMS,
        cost_estimate=cost(1, 1),
        name="tables",
    )(place, lengths)


def pack_kernel(count, *refs):
    out_ref = refs[-1]
    pieces, share = out_ref.shape[0], out_ref.shape[-1]
    for t in range(count):
        for f in range(pieces):
            out_ref[f, 0, t] = refs[t][0, 0, :, f * share : (f + 1) * share]


def first_tile(array):
    lead = len(array.shape) - 2
    return pl.BlockSpec((1,) * lead + (16, 128), lambda *_: (0,) * (lead + 2))


def pack(states, chunk, pieces, after=()):
    low, high = chunk
    _, _, piece, width = states[0].shape
    share = width // pieces
    count = len(states)
    shape = (pieces, high - low, count, piece, share)
    return pl.pallas_call(
        lambda *refs: pack_kernel(count, *refs),
        grid=(high - low,),
        in_specs=[
            *[pl.BlockSpec((1, 1, piece, width), lambda r: (0, r + low, 0, 0))] * count,
            *[first_tile(array) for array in after],
        ],
        out_specs=pl.BlockSpec((pieces, 1, count, piece, share), lambda r: (0, r, 0, 0, 0)),
        out_shape=pltpu.HBM(shape, jnp.bfloat16),
        compiler_params=PARAMS,
        cost_estimate=cost(1, 1),
        name="pack",
    )(*[pltpu.with_memory_space_constraint(state, pltpu.HBM) for state in states], *after)


def attend_kernel(side_ref, first_ref, here_ref, ahead_ref, q_ref, next_q_ref, own_ref, other_ref, *refs):
    out_ref, sent_ref, contexts = refs[-3:]
    factor = math.log2(math.e) / math.sqrt(HEAD)
    pieces, _, _, piece, features = q_ref.shape
    block = SPAN // 2

    def rows(ref, index, start, stop, lanes):
        parts = []
        for ring in range(2):
            low, high = max(start - ring * SPAN, 0), min(stop - ring * SPAN, SPAN)
            if low < high:
                some = ref[ring][low // piece : high // piece, 0, index, :, lanes]
                parts.append(some.reshape(high - low, HEAD))
        return parts[0] if len(parts) == 1 else jnp.concatenate(parts, 0)

    def attend_rings(states, queries, spots, keep_at):
        for spot in spots:
            start, stop = max(0, spot - SPAN), spot + block
            key = lax.broadcasted_iota(jnp.int32, (stop - start, block), 0) + start
            here = lax.broadcasted_iota(jnp.int32, (stop - start, block), 1) + spot
            keep = (key >= first_ref[0, :, spot:stop]) & (key <= here)
            bias = jnp.where(keep, 0.0, -1e30)
            for h in range(features // HEAD):
                lanes = slice(h * HEAD, (h + 1) * HEAD)
                scores = dot(rows(states, 0, start, stop, lanes), rows(queries, 0, spot, stop, lanes), NT) + bias
                top = jnp.max(scores, axis=0, keepdims=True)
                raised = jnp.exp2((scores - top) * factor)
                total = jnp.sum(raised, axis=0, keepdims=True)
                weights = (raised * (1.0 / total)).astype(jnp.bfloat16)
                context = dot(weights, rows(states, 1, start, stop, lanes), TN)
                keep_at(slice(spot, stop), lanes, context.astype(jnp.bfloat16))

    @pl.when(side_ref[0] == 0)
    def _():
        def store(at, lanes, context):
            out_ref[0, at.start - SPAN : at.stop - SPAN, lanes] = context

        attend_rings((other_ref, own_ref), (None, q_ref), (SPAN, SPAN + block), store)
        sent_ref[...] = jnp.zeros_like(sent_ref)

    @pl.when(side_ref[0] != 0)
    def _():
        def store(at, lanes, context):
            contexts[at, lanes] = context

        attend_rings((own_ref, other_ref), (q_ref, next_q_ref), (0, block, SPAN, SPAN + block), store)
        source = lax.broadcasted_iota(jnp.int32, (2 * SPAN, SPAN), 0)
        for index, ref in ((here_ref[0], out_ref), (ahead_ref[0], sent_ref)):
            chosen = jnp.where(source == index, 1.0, 0.0).astype(jnp.bfloat16)
            ref[0] = dot(chosen, contexts[...], TN).astype(jnp.bfloat16)


def attend(side, first, here, ahead, q, next_q, own, other, chunk, base, after, weight):
    pieces, _, _, piece, features = own.shape
    low, high = chunk
    rows = high - low

    def line(array):
        return pl.BlockSpec((1, 1, array.shape[2]), lambda r: (r + low, 0, 0))

    def states(array, at):
        return pl.BlockSpec((pieces, 1, array.shape[2], piece, features), lambda r: (0, r + at, 0, 0, 0))

    block = pl.BlockSpec((1, SPAN, features), lambda r: (r, 0, 0))
    return pl.pallas_call(
        attend_kernel,
        grid=(rows,),
        in_specs=[
            pl.BlockSpec(memory_space=pltpu.SMEM),
            line(first),
            line(here),
            line(ahead),
            states(q, low),
            states(next_q, low),
            states(own, low - base),
            states(other, low - base),
            *[first_tile(array) for array in after],
        ],
        out_specs=[block, block],
        out_shape=[jax.ShapeDtypeStruct((rows, SPAN, features), jnp.bfloat16)] * 2,
        scratch_shapes=[pltpu.VMEM((2 * SPAN, features), jnp.bfloat16)],
        compiler_params=pltpu.CompilerParams(vmem_limit_bytes=28 * 2**20),
        cost_estimate=cost(rows * weight, 1),
        name="attend",
    )(side, first, here, ahead, q, next_q, own, other, *after)


def join_kernel(side_ref, mine_ref, other_ref, weight_ref, second_ref, *refs):
    out_ref = refs[-1]
    rows, tokens, depth = mine_ref.shape
    pieces, _, piece, wide = out_ref.shape
    weight = weight_ref[...].reshape(depth, wide)
    second = second_ref[...].reshape(depth, wide)
    for r in range(rows):
        total = dot(mine_ref[r], weight) + dot(other_ref[r], second)
        out_ref[:, r] = total.astype(jnp.bfloat16).reshape(pieces, piece, wide)


def join(side, mine, other, weight, pieces, after=()):
    rows, tokens, depth = mine.shape
    heads, _, head, units = weight.shape
    wide = units // 2
    whole = pl.BlockSpec((rows, tokens, depth), lambda n, side: (0, 0, 0))
    return pl.pallas_call(
        join_kernel,
        grid_spec=pltpu.PrefetchScalarGridSpec(
            num_scalar_prefetch=1,
            grid=(units // wide,),
            in_specs=[
                whole,
                whole,
                pl.BlockSpec((heads, 1, head, wide), lambda n, side: (0, side[0], 0, n)),
                pl.BlockSpec((heads, 1, head, wide), lambda n, side: (0, 1 - side[0], 0, n)),
                *[first_tile(array) for array in after],
            ],
            out_specs=pl.BlockSpec((pieces, rows, tokens // pieces, wide), lambda n, side: (0, 0, 0, n)),
        ),
        out_shape=jax.ShapeDtypeStruct((pieces, rows, tokens // pieces, units), jnp.bfloat16),
        compiler_params=PARAMS,
        cost_estimate=cost(1, 1),
        name="join",
    )(side, mine, other, weight, weight, *after)


def body(queries, key_states, value_vectors, hypothesis_lengths, join_weight):
    _, rows, piece, width = queries.shape
    pieces = SPAN // piece
    share = width // pieces
    side = lax.axis_index("dir")
    ring = lax.axis_index("y") * 8 + lax.axis_index("z")

    def exchange(parts):
        return lax.all_to_all(parts, "x", split_axis=0, concat_axis=0, tiled=True)

    to_left = [(RINGS + c + 1, RINGS + c) for c in range(RINGS - 1)]
    to_right = [(RINGS + c, RINGS + c + 1) for c in range(RINGS - 1)]
    outward = [(c, c + 1) for c in range(RINGS - 1)] + to_left

    def passed(array, pairs):
        return lax.ppermute(array, ("dir", "y", "z"), pairs)

    turned = lax.ppermute(
        join_weight.reshape(piece, -1), ("y", "x"), [(y * 4 + x, x * 4 + y) for y in range(4) for x in range(4)]
    )
    weight = lax.all_gather(turned, ("z", "y"), tiled=True)
    units = weight.shape[1]
    weight_rows = pltpu.with_memory_space_constraint(weight.reshape(share // HEAD, 2, HEAD, units), pltpu.HBM)
    base = (ring - 1 + side) * SPAN
    lines = tables(base[None], hypothesis_lengths)

    both = (key_states, value_vectors)
    own_early = exchange(pack(both, CHUNKS[0], pieces))
    other_early = passed(own_early, outward)
    q = exchange(pack((queries,), (0, rows), pieces, (own_early, turned)))
    next_q = passed(q, to_left)
    own_late = exchange(pack(both, CHUNKS[1], pieces, (q, other_early)))
    other_late = passed(own_late, outward)

    def contexts(own, other, chunk, low, after=(), weight=LONG):
        return attend(side[None], *lines, q, next_q, own, other, chunk, low, after, weight)

    def swapped(mine, ahead):
        mine = mine + passed(ahead, to_right)
        return mine, lax.ppermute(mine, "dir", [(0, 1), (1, 0)])

    def joined_part(mine, partner, after=()):
        return join(side[None], mine, partner, weight_rows, pieces, after)

    def gated(arrived):
        total = jnp.sum(arrived.astype(jnp.float32), axis=0)
        return (jax.nn.silu(total[..., : units // 2]) * total[..., units // 2 :]).astype(jnp.bfloat16)

    early = contexts(own_early, other_early, (0, 2), 0, (own_late,))
    late = contexts(own_late, other_late, (2, 4), 2, (early[1],))
    partial_value = joined_part(*swapped(*early), ())
    arrived = [exchange(partial_value), exchange(joined_part(*swapped(*late), (partial_value,)))]
    joined = [gated(one) for one in arrived]
    return jnp.concatenate(joined)


def solution(mesh):
    fine = Mesh(mesh.devices.reshape(2, 4, 8, 4), ("dir", "y", "z", "x"))
    states = P("dir", None, ("y", "z", "x"), None)
    return jax.shard_map(
        body,
        mesh=fine,
        in_specs=(states, states, states, P(), P(("y", "z", "x"), None, "dir")),
        out_specs=P(None, ("y", "z", "x"), "dir"),
        check_vma=False,
    )
```

```python
import math

import jax
import jax.numpy as jnp
from jax import lax
from jax.experimental import pallas as pl
from jax.experimental.pallas import tpu as pltpu
from jax.sharding import Mesh
from jax.sharding import PartitionSpec as P

HEAD = 128
SPAN = 256
HALF = SPAN // 2
RINGS = 32
LONG = 10**10
CHUNKS = ((0, 2), (2, 4))
NT = (((1,), (1,)), ((), ()))
NN = (((1,), (0,)), ((), ()))
TN = (((0,), (0,)), ((), ()))
PARAMS = pltpu.CompilerParams(vmem_limit_bytes=16 * 2**20)


def dot(a, b, dims=NN):
    return lax.dot_general(a, b, dims, preferred_element_type=jnp.float32)


def cost(flops, nbytes):
    return pl.CostEstimate(flops=flops, bytes_accessed=nbytes, transcendentals=0)


def table_kernel(place_ref, lengths_ref, first_ref, here_ref, ahead_ref):
    rows, count = lengths_ref.shape
    base = place_ref[0]
    lengths = lengths_ref[...].astype(jnp.float32)
    upto = lax.broadcasted_iota(jnp.int32, (count, count), 1) <= lax.broadcasted_iota(jnp.int32, (count, count), 0)
    before = lax.broadcasted_iota(jnp.int32, (count, count), 1) < lax.broadcasted_iota(jnp.int32, (count, count), 0)
    lengths = lengths.astype(jnp.bfloat16)
    ends = dot(jnp.where(upto, 1.0, 0.0).astype(jnp.bfloat16), lengths, NT)
    starts = dot(jnp.where(before, 1.0, 0.0).astype(jnp.bfloat16), lengths, NT)
    place = lax.broadcasted_iota(jnp.int32, (1, 2 * SPAN), 1)
    at = (place + base).astype(jnp.float32)
    for r in range(rows):
        start, stop = starts[:, r : r + 1], ends[:, r : r + 1]
        first = jnp.max(jnp.where(start <= at, start, 0.0), axis=0, keepdims=True).astype(jnp.int32) - base
        end = jnp.min(jnp.where(stop > at, stop, 1e6), axis=0, keepdims=True).astype(jnp.int32) - base
        mirror = jnp.where((first >= 0) & (first < SPAN), first + end - 1 - place, -1)
        first_ref[r] = first
        here_ref[r] = mirror[:, :SPAN]
        ahead_ref[r] = mirror[:, SPAN:]


def tables(place, lengths):
    rows = lengths.shape[0]
    return pl.pallas_call(
        table_kernel,
        in_specs=[pl.BlockSpec(memory_space=pltpu.SMEM), pl.BlockSpec(memory_space=pltpu.VMEM)],
        out_shape=[jax.ShapeDtypeStruct((rows, 1, n), jnp.int32) for n in (2 * SPAN, SPAN, SPAN)],
        compiler_params=PARAMS,
        cost_estimate=cost(1, 1),
        name="tables",
    )(place, lengths)


def pack_kernel(count, *refs):
    out_ref = refs[-1]
    pieces, share = out_ref.shape[0], out_ref.shape[-1]
    for t in range(count):
        for f in range(pieces):
            out_ref[f, 0, t] = refs[t][0, 0, :, f * share : (f + 1) * share]


def first_tile(array):
    lead = len(array.shape) - 2
    return pl.BlockSpec((1,) * lead + (16, 128), lambda *_: (0,) * (lead + 2))


def pack(states, chunk, pieces, after=()):
    low, high = chunk
    _, _, piece, width = states[0].shape
    share = width // pieces
    count = len(states)
    shape = (pieces, high - low, count, piece, share)
    return pl.pallas_call(
        lambda *refs: pack_kernel(count, *refs),
        grid=(high - low,),
        in_specs=[
            *[pl.BlockSpec((1, 1, piece, width), lambda r: (0, r + low, 0, 0))] * count,
            *[first_tile(array) for array in after],
        ],
        out_specs=pl.BlockSpec((pieces, 1, count, piece, share), lambda r: (0, r, 0, 0, 0)),
        out_shape=pltpu.HBM(shape, jnp.bfloat16),
        compiler_params=PARAMS,
        cost_estimate=cost(2*10**9, 1),
        name="pack",
    )(*[pltpu.with_memory_space_constraint(state, pltpu.HBM) for state in states], *after)


def attend_kernel(side_ref, first_ref, here_ref, ahead_ref, q_ref, next_q_ref, own_ref, other_ref, *refs):
    out_ref, sent_ref, contexts = refs[-3:]
    factor = math.log2(math.e) / math.sqrt(HEAD)
    pieces, _, _, piece, features = q_ref.shape
    block = SPAN // 2

    def rows(ref, index, start, stop, lanes):
        parts = []
        for ring in range(2):
            low, high = max(start - ring * SPAN, 0), min(stop - ring * SPAN, SPAN)
            if low < high:
                some = ref[ring][low // piece : high // piece, 0, index, :, lanes]
                parts.append(some.reshape(high - low, HEAD))
        return parts[0] if len(parts) == 1 else jnp.concatenate(parts, 0)

    def attend_rings(states, queries, spots, keep_at):
        for spot in spots:
            start, stop = max(0, spot - SPAN), spot + block
            key = lax.broadcasted_iota(jnp.int32, (stop - start, block), 0) + start
            here = lax.broadcasted_iota(jnp.int32, (stop - start, block), 1) + spot
            keep = (key >= first_ref[0, :, spot:stop]) & (key <= here)
            bias = jnp.where(keep, 0.0, -1e30)
            for h in range(features // HEAD):
                lanes = slice(h * HEAD, (h + 1) * HEAD)
                scores = dot(rows(states, 0, start, stop, lanes), rows(queries, 0, spot, stop, lanes), NT) + bias
                top = jnp.max(scores, axis=0, keepdims=True)
                raised = jnp.exp2((scores - top) * factor)
                total = jnp.sum(raised, axis=0, keepdims=True)
                weights = (raised * (1.0 / total)).astype(jnp.bfloat16)
                context = dot(weights, rows(states, 1, start, stop, lanes), TN)
                keep_at(slice(spot, stop), lanes, context.astype(jnp.bfloat16))

    @pl.when(side_ref[0] == 0)
    def _():
        def store(at, lanes, context):
            out_ref[0, at.start - SPAN : at.stop - SPAN, lanes] = context

        attend_rings((other_ref, own_ref), (None, q_ref), (SPAN, SPAN + block), store)
        sent_ref[...] = jnp.zeros_like(sent_ref)

    @pl.when(side_ref[0] != 0)
    def _():
        def store(at, lanes, context):
            contexts[at, lanes] = context

        attend_rings((own_ref, other_ref), (q_ref, next_q_ref), (0, block, SPAN, SPAN + block), store)
        source = lax.broadcasted_iota(jnp.int32, (2 * SPAN, SPAN), 0)
        for index, ref in ((here_ref[0], out_ref), (ahead_ref[0], sent_ref)):
            chosen = jnp.where(source == index, 1.0, 0.0).astype(jnp.bfloat16)
            ref[0] = dot(chosen, contexts[...], TN).astype(jnp.bfloat16)


def attend(side, first, here, ahead, q, next_q, own, other, chunk, base, after, weight):
    pieces, _, _, piece, features = own.shape
    low, high = chunk
    rows = high - low

    def line(array):
        return pl.BlockSpec((1, 1, array.shape[2]), lambda r: (r + low, 0, 0))

    def states(array, at):
        return pl.BlockSpec((pieces, 1, array.shape[2], piece, features), lambda r: (0, r + at, 0, 0, 0))

    block = pl.BlockSpec((1, SPAN, features), lambda r: (r, 0, 0))
    return pl.pallas_call(
        attend_kernel,
        grid=(rows,),
        in_specs=[
            pl.BlockSpec(memory_space=pltpu.SMEM),
            line(first),
            line(here),
            line(ahead),
            states(q, low),
            states(next_q, low),
            states(own, low - base),
            states(other, low - base),
            *[first_tile(array) for array in after],
        ],
        out_specs=[block, block],
        out_shape=[jax.ShapeDtypeStruct((rows, SPAN, features), jnp.bfloat16)] * 2,
        scratch_shapes=[pltpu.VMEM((2 * SPAN, features), jnp.bfloat16)],
        compiler_params=pltpu.CompilerParams(vmem_limit_bytes=28 * 2**20),
        cost_estimate=cost(rows * weight, 1),
        name="attend",
    )(side, first, here, ahead, q, next_q, own, other, *after)


def join_kernel(side_ref, mine_ref, other_ref, weight_ref, second_ref, *refs):
    out_ref = refs[-1]
    rows, tokens, depth = mine_ref.shape
    pieces, _, piece, wide = out_ref.shape
    weight = weight_ref[...].reshape(depth, wide)
    second = second_ref[...].reshape(depth, wide)
    for r in range(rows):
        total = dot(mine_ref[r], weight) + dot(other_ref[r], second)
        out_ref[:, r] = total.astype(jnp.bfloat16).reshape(pieces, piece, wide)


def join(side, mine, other, weight, pieces, after=()):
    rows, tokens, depth = mine.shape
    heads, _, head, units = weight.shape
    wide = units // 2
    whole = pl.BlockSpec((rows, tokens, depth), lambda n, side: (0, 0, 0))
    return pl.pallas_call(
        join_kernel,
        grid_spec=pltpu.PrefetchScalarGridSpec(
            num_scalar_prefetch=1,
            grid=(units // wide,),
            in_specs=[
                whole,
                whole,
                pl.BlockSpec((heads, 1, head, wide), lambda n, side: (0, side[0], 0, n)),
                pl.BlockSpec((heads, 1, head, wide), lambda n, side: (0, 1 - side[0], 0, n)),
                *[first_tile(array) for array in after],
            ],
            out_specs=pl.BlockSpec((pieces, rows, tokens // pieces, wide), lambda n, side: (0, 0, 0, n)),
        ),
        out_shape=jax.ShapeDtypeStruct((pieces, rows, tokens // pieces, units), jnp.bfloat16),
        compiler_params=PARAMS,
        cost_estimate=cost(1, 1),
        name="join",
    )(side, mine, other, weight, weight, *after)


def body(queries, key_states, value_vectors, hypothesis_lengths, join_weight):
    _, rows, piece, width = queries.shape
    pieces = SPAN // piece
    share = width // pieces
    side = lax.axis_index("dir")
    ring = lax.axis_index("y") * 8 + lax.axis_index("z")

    def behind(array, *others):
        return lax.optimization_barrier((array, *others))[0]

    def exchange(parts):
        return lax.all_to_all(parts, "x", split_axis=0, concat_axis=0, tiled=True)

    to_left = [(RINGS + c + 1, RINGS + c) for c in range(RINGS - 1)]
    to_right = [(RINGS + c, RINGS + c + 1) for c in range(RINGS - 1)]
    outward = [(c, c + 1) for c in range(RINGS - 1)] + to_left

    def passed(array, pairs):
        return lax.ppermute(array, ("dir", "y", "z"), pairs)

    turned = lax.ppermute(
        join_weight.reshape(piece, -1), ("y", "x"), [(y * 4 + x, x * 4 + y) for y in range(4) for x in range(4)]
    )
    weight = lax.all_gather(turned, ("z", "y"), tiled=True)
    units = weight.shape[1]
    weight_rows = pltpu.with_memory_space_constraint(weight.reshape(share // HEAD, 2, HEAD, units), pltpu.HBM)
    base = (ring - 1 + side) * SPAN
    lines = tables(base[None], hypothesis_lengths)

    both = (key_states, value_vectors)
    own_early = exchange(pack(both, CHUNKS[0], pieces))
    other_early = passed(own_early, outward)
    q = exchange(pack((queries,), (0, rows), pieces, (own_early, turned)))
    next_q = passed(q, to_left)
    own_late = exchange(pack(both, CHUNKS[1], pieces, (q, other_early)))
    other_late = passed(own_late, outward)

    def contexts(own, other, chunk, low, after=(), weight=LONG):
        return attend(side[None], *lines, q, next_q, own, other, chunk, low, after, weight)

    def swapped(mine, ahead):
        mine = mine + passed(ahead, to_right)
        return mine, lax.ppermute(mine, "dir", [(0, 1), (1, 0)])

    def joined_part(mine, partner, after=()):
        return join(side[None], mine, partner, weight_rows, pieces, after)

    def gated(arrived):
        total = jnp.sum(arrived.astype(jnp.float32), axis=0)
        return (jax.nn.silu(total[..., : units // 2]) * total[..., units // 2 :]).astype(jnp.bfloat16)

    early = contexts(own_early, other_early, (0, 2), 0, (own_late,))
    late = contexts(own_late, other_late, (2, 3), 2, (early[1],))
    partial_early = joined_part(*swapped(*early))
    last = contexts(own_late, other_late, (3, 4), 2, (late[1], partial_early))
    early = exchange(partial_early)
    partial_late = joined_part(*swapped(*late), ())
    late = exchange(behind(partial_late, early))
    last = exchange(joined_part(*swapped(*last), (partial_late,)))
    joined = [gated(one) for one in (early, late, last)]
    return jnp.concatenate(joined)


def solution(mesh):
    fine = Mesh(mesh.devices.reshape(2, 4, 8, 4), ("dir", "y", "z", "x"))
    states = P("dir", None, ("y", "z", "x"), None)
    return jax.shard_map(
        body,
        mesh=fine,
        in_specs=(states, states, states, P(), P(("y", "z", "x"), None, "dir")),
        out_specs=P(None, ("y", "z", "x"), "dir"),
        check_vma=False,
    )
```

```python
import math

import jax
import jax.numpy as jnp
from jax import lax
from jax.experimental import pallas as pl
from jax.experimental.pallas import tpu as pltpu
from jax.sharding import Mesh
from jax.sharding import PartitionSpec as P

HEAD = 128
SPAN = 256
HALF = SPAN // 2
RINGS = 32
LONG = 1
CHUNKS = ((0, 2), (2, 4))
NT = (((1,), (1,)), ((), ()))
NN = (((1,), (0,)), ((), ()))
TN = (((0,), (0,)), ((), ()))
PARAMS = pltpu.CompilerParams(vmem_limit_bytes=16 * 2**20)


def dot(a, b, dims=NN):
    return lax.dot_general(a, b, dims, preferred_element_type=jnp.float32)


def cost(flops, nbytes):
    return pl.CostEstimate(flops=flops, bytes_accessed=nbytes, transcendentals=0)


def table_kernel(place_ref, lengths_ref, first_ref, here_ref, ahead_ref):
    rows, count = lengths_ref.shape
    base = place_ref[0]
    lengths = lengths_ref[...].astype(jnp.float32)
    upto = lax.broadcasted_iota(jnp.int32, (count, count), 1) <= lax.broadcasted_iota(jnp.int32, (count, count), 0)
    before = lax.broadcasted_iota(jnp.int32, (count, count), 1) < lax.broadcasted_iota(jnp.int32, (count, count), 0)
    lengths = lengths.astype(jnp.bfloat16)
    ends = dot(jnp.where(upto, 1.0, 0.0).astype(jnp.bfloat16), lengths, NT)
    starts = dot(jnp.where(before, 1.0, 0.0).astype(jnp.bfloat16), lengths, NT)
    place = lax.broadcasted_iota(jnp.int32, (1, 2 * SPAN), 1)
    at = (place + base).astype(jnp.float32)
    for r in range(rows):
        start, stop = starts[:, r : r + 1], ends[:, r : r + 1]
        first = jnp.max(jnp.where(start <= at, start, 0.0), axis=0, keepdims=True).astype(jnp.int32) - base
        end = jnp.min(jnp.where(stop > at, stop, 1e6), axis=0, keepdims=True).astype(jnp.int32) - base
        mirror = jnp.where((first >= 0) & (first < SPAN), first + end - 1 - place, -1)
        first_ref[r] = first
        here_ref[r] = mirror[:, :SPAN]
        ahead_ref[r] = mirror[:, SPAN:]


def tables(place, lengths):
    rows = lengths.shape[0]
    return pl.pallas_call(
        table_kernel,
        in_specs=[pl.BlockSpec(memory_space=pltpu.SMEM), pl.BlockSpec(memory_space=pltpu.VMEM)],
        out_shape=[jax.ShapeDtypeStruct((rows, 1, n), jnp.int32) for n in (2 * SPAN, SPAN, SPAN)],
        compiler_params=PARAMS,
        cost_estimate=cost(1, 1),
        name="tables",
    )(place, lengths)


def pack_kernel(count, *refs):
    out_ref = refs[-1]
    pieces, share = out_ref.shape[0], out_ref.shape[-1]
    for t in range(count):
        for f in range(pieces):
            out_ref[f, 0, t] = refs[t][0, 0, :, f * share : (f + 1) * share]


def first_tile(array):
    lead = len(array.shape) - 2
    return pl.BlockSpec((1,) * lead + (16, 128), lambda *_: (0,) * (lead + 2))


def pack(states, chunk, pieces, after=()):
    low, high = chunk
    _, _, piece, width = states[0].shape
    share = width // pieces
    count = len(states)
    shape = (pieces, high - low, count, piece, share)
    return pl.pallas_call(
        lambda *refs: pack_kernel(count, *refs),
        grid=(high - low,),
        in_specs=[
            *[pl.BlockSpec((1, 1, piece, width), lambda r: (0, r + low, 0, 0))] * count,
            *[first_tile(array) for array in after],
        ],
        out_specs=pl.BlockSpec((pieces, 1, count, piece, share), lambda r: (0, r, 0, 0, 0)),
        out_shape=pltpu.HBM(shape, jnp.bfloat16),
        compiler_params=PARAMS,
        cost_estimate=cost(2*10**9, 1),
        name="pack",
    )(*[pltpu.with_memory_space_constraint(state, pltpu.HBM) for state in states], *after)


def attend_kernel(side_ref, first_ref, here_ref, ahead_ref, q_ref, next_q_ref, own_ref, other_ref, *refs):
    out_ref, sent_ref, contexts = refs[-3:]
    factor = math.log2(math.e) / math.sqrt(HEAD)
    pieces, _, _, piece, features = q_ref.shape
    block = SPAN // 2

    def rows(ref, index, start, stop, lanes):
        parts = []
        for ring in range(2):
            low, high = max(start - ring * SPAN, 0), min(stop - ring * SPAN, SPAN)
            if low < high:
                some = ref[ring][low // piece : high // piece, 0, index, :, lanes]
                parts.append(some.reshape(high - low, HEAD))
        return parts[0] if len(parts) == 1 else jnp.concatenate(parts, 0)

    def attend_rings(states, queries, spots, keep_at):
        for spot in spots:
            start, stop = max(0, spot - SPAN), spot + block
            key = lax.broadcasted_iota(jnp.int32, (stop - start, block), 0) + start
            here = lax.broadcasted_iota(jnp.int32, (stop - start, block), 1) + spot
            keep = (key >= first_ref[0, :, spot:stop]) & (key <= here)
            bias = jnp.where(keep, 0.0, -1e30)
            for h in range(features // HEAD):
                lanes = slice(h * HEAD, (h + 1) * HEAD)
                scores = dot(rows(states, 0, start, stop, lanes), rows(queries, 0, spot, stop, lanes), NT) + bias
                top = jnp.max(scores, axis=0, keepdims=True)
                raised = jnp.exp2((scores - top) * factor)
                total = jnp.sum(raised, axis=0, keepdims=True)
                weights = (raised * (1.0 / total)).astype(jnp.bfloat16)
                context = dot(weights, rows(states, 1, start, stop, lanes), TN)
                keep_at(slice(spot, stop), lanes, context.astype(jnp.bfloat16))

    @pl.when(side_ref[0] == 0)
    def _():
        def store(at, lanes, context):
            out_ref[0, at.start - SPAN : at.stop - SPAN, lanes] = context

        attend_rings((other_ref, own_ref), (None, q_ref), (SPAN, SPAN + block), store)
        sent_ref[...] = jnp.zeros_like(sent_ref)

    @pl.when(side_ref[0] != 0)
    def _():
        def store(at, lanes, context):
            contexts[at, lanes] = context

        attend_rings((own_ref, other_ref), (q_ref, next_q_ref), (0, block, SPAN, SPAN + block), store)
        source = lax.broadcasted_iota(jnp.int32, (2 * SPAN, SPAN), 0)
        for index, ref in ((here_ref[0], out_ref), (ahead_ref[0], sent_ref)):
            chosen = jnp.where(source == index, 1.0, 0.0).astype(jnp.bfloat16)
            ref[0] = dot(chosen, contexts[...], TN).astype(jnp.bfloat16)


def attend(side, first, here, ahead, q, next_q, own, other, chunk, base, after, weight):
    pieces, _, _, piece, features = own.shape
    low, high = chunk
    rows = high - low

    def line(array):
        return pl.BlockSpec((1, 1, array.shape[2]), lambda r: (r + low, 0, 0))

    def states(array, at):
        return pl.BlockSpec((pieces, 1, array.shape[2], piece, features), lambda r: (0, r + at, 0, 0, 0))

    block = pl.BlockSpec((1, SPAN, features), lambda r: (r, 0, 0))
    return pl.pallas_call(
        attend_kernel,
        grid=(rows,),
        in_specs=[
            pl.BlockSpec(memory_space=pltpu.SMEM),
            line(first),
            line(here),
            line(ahead),
            states(q, low),
            states(next_q, low),
            states(own, low - base),
            states(other, low - base),
            *[first_tile(array) for array in after],
        ],
        out_specs=[block, block],
        out_shape=[jax.ShapeDtypeStruct((rows, SPAN, features), jnp.bfloat16)] * 2,
        scratch_shapes=[pltpu.VMEM((2 * SPAN, features), jnp.bfloat16)],
        compiler_params=pltpu.CompilerParams(vmem_limit_bytes=28 * 2**20),
        cost_estimate=cost(rows * weight, 1),
        name="attend",
    )(side, first, here, ahead, q, next_q, own, other, *after)


def join_kernel(side_ref, mine_ref, other_ref, weight_ref, second_ref, *refs):
    out_ref = refs[-1]
    rows, tokens, depth = mine_ref.shape
    pieces, _, piece, wide = out_ref.shape
    weight = weight_ref[...].reshape(depth, wide)
    second = second_ref[...].reshape(depth, wide)
    for r in range(rows):
        total = dot(mine_ref[r], weight) + dot(other_ref[r], second)
        out_ref[:, r] = total.astype(jnp.bfloat16).reshape(pieces, piece, wide)


def join(side, mine, other, weight, pieces, after=()):
    rows, tokens, depth = mine.shape
    heads, _, head, units = weight.shape
    wide = units // 2
    whole = pl.BlockSpec((rows, tokens, depth), lambda n, side: (0, 0, 0))
    return pl.pallas_call(
        join_kernel,
        grid_spec=pltpu.PrefetchScalarGridSpec(
            num_scalar_prefetch=1,
            grid=(units // wide,),
            in_specs=[
                whole,
                whole,
                pl.BlockSpec((heads, 1, head, wide), lambda n, side: (0, side[0], 0, n)),
                pl.BlockSpec((heads, 1, head, wide), lambda n, side: (0, 1 - side[0], 0, n)),
                *[first_tile(array) for array in after],
            ],
            out_specs=pl.BlockSpec((pieces, rows, tokens // pieces, wide), lambda n, side: (0, 0, 0, n)),
        ),
        out_shape=jax.ShapeDtypeStruct((pieces, rows, tokens // pieces, units), jnp.bfloat16),
        compiler_params=PARAMS,
        cost_estimate=cost(1, 1),
        name="join",
    )(side, mine, other, weight, weight, *after)


def body(queries, key_states, value_vectors, hypothesis_lengths, join_weight):
    _, rows, piece, width = queries.shape
    pieces = SPAN // piece
    share = width // pieces
    side = lax.axis_index("dir")
    ring = lax.axis_index("y") * 8 + lax.axis_index("z")

    def behind(array, *others):
        return lax.optimization_barrier((array, *others))[0]

    def exchange(parts):
        return lax.all_to_all(parts, "x", split_axis=0, concat_axis=0, tiled=True)

    to_left = [(RINGS + c + 1, RINGS + c) for c in range(RINGS - 1)]
    to_right = [(RINGS + c, RINGS + c + 1) for c in range(RINGS - 1)]
    outward = [(c, c + 1) for c in range(RINGS - 1)] + to_left

    def passed(array, pairs):
        return lax.ppermute(array, ("dir", "y", "z"), pairs)

    turned = lax.ppermute(
        join_weight.reshape(piece, -1), ("y", "x"), [(y * 4 + x, x * 4 + y) for y in range(4) for x in range(4)]
    )
    weight = lax.all_gather(turned, ("z", "y"), tiled=True)
    units = weight.shape[1]
    weight_rows = pltpu.with_memory_space_constraint(weight.reshape(share // HEAD, 2, HEAD, units), pltpu.HBM)
    base = (ring - 1 + side) * SPAN
    lines = tables(base[None], hypothesis_lengths)

    both = (key_states, value_vectors)
    own_early = exchange(pack(both, CHUNKS[0], pieces))
    other_early = passed(own_early, outward)
    own_late = exchange(pack(both, CHUNKS[1], pieces, (own_early, turned)))
    other_late = passed(own_late, outward)
    q = exchange(pack((queries,), (0, rows), pieces, (own_late, other_early)))
    next_q = passed(q, to_left)

    def contexts(own, other, chunk, low, after=(), weight=LONG):
        return attend(side[None], *lines, q, next_q, own, other, chunk, low, after, weight)

    def swapped(mine, ahead):
        mine = mine + passed(ahead, to_right)
        return mine, lax.ppermute(mine, "dir", [(0, 1), (1, 0)])

    def joined_part(mine, partner, after=()):
        return join(side[None], mine, partner, weight_rows, pieces, after)

    def gated(arrived):
        total = jnp.sum(arrived.astype(jnp.float32), axis=0)
        return (jax.nn.silu(total[..., : units // 2]) * total[..., units // 2 :]).astype(jnp.bfloat16)

    early = contexts(own_early, other_early, (0, 2), 0, (other_late,))
    late = contexts(own_late, other_late, (2, 3), 2, (early[1],))
    partial_early = joined_part(*swapped(*early))
    last = contexts(own_late, other_late, (3, 4), 2, (late[1], partial_early))
    early = exchange(partial_early)
    partial_late = joined_part(*swapped(*late), ())
    late = exchange(behind(partial_late, early))
    last = exchange(joined_part(*swapped(*last), (partial_late,)))
    joined = [gated(one) for one in (early, late, last)]
    return jnp.concatenate(joined)


def solution(mesh):
    fine = Mesh(mesh.devices.reshape(2, 4, 8, 4), ("dir", "y", "z", "x"))
    states = P("dir", None, ("y", "z", "x"), None)
    return jax.shard_map(
        body,
        mesh=fine,
        in_specs=(states, states, states, P(), P(("y", "z", "x"), None, "dir")),
        out_specs=P(None, ("y", "z", "x"), "dir"),
        check_vma=False,
    )
```

```python
import math

import jax
import jax.numpy as jnp
from jax import lax
from jax.experimental import pallas as pl
from jax.experimental.pallas import tpu as pltpu
from jax.sharding import Mesh
from jax.sharding import PartitionSpec as P

HEAD = 128
SPAN = 256
HALF = SPAN // 2
RINGS = 32
LONG = 10**10
CHUNKS = ((0, 2), (2, 4))
NT = (((1,), (1,)), ((), ()))
NN = (((1,), (0,)), ((), ()))
TN = (((0,), (0,)), ((), ()))
PARAMS = pltpu.CompilerParams(vmem_limit_bytes=16 * 2**20)


def dot(a, b, dims=NN):
    return lax.dot_general(a, b, dims, preferred_element_type=jnp.float32)


def cost(flops, nbytes):
    return pl.CostEstimate(flops=flops, bytes_accessed=nbytes, transcendentals=0)


def table_kernel(place_ref, lengths_ref, first_ref, here_ref, ahead_ref):
    rows, count = lengths_ref.shape
    base = place_ref[0]
    lengths = lengths_ref[...].astype(jnp.float32)
    upto = lax.broadcasted_iota(jnp.int32, (count, count), 1) <= lax.broadcasted_iota(jnp.int32, (count, count), 0)
    before = lax.broadcasted_iota(jnp.int32, (count, count), 1) < lax.broadcasted_iota(jnp.int32, (count, count), 0)
    lengths = lengths.astype(jnp.bfloat16)
    ends = dot(jnp.where(upto, 1.0, 0.0).astype(jnp.bfloat16), lengths, NT)
    starts = dot(jnp.where(before, 1.0, 0.0).astype(jnp.bfloat16), lengths, NT)
    place = lax.broadcasted_iota(jnp.int32, (1, 2 * SPAN), 1)
    at = (place + base).astype(jnp.float32)
    for r in range(rows):
        start, stop = starts[:, r : r + 1], ends[:, r : r + 1]
        first = jnp.max(jnp.where(start <= at, start, 0.0), axis=0, keepdims=True).astype(jnp.int32) - base
        end = jnp.min(jnp.where(stop > at, stop, 1e6), axis=0, keepdims=True).astype(jnp.int32) - base
        mirror = jnp.where((first >= 0) & (first < SPAN), first + end - 1 - place, -1)
        first_ref[r] = first
        here_ref[r] = mirror[:, :SPAN]
        ahead_ref[r] = mirror[:, SPAN:]


def tables(place, lengths):
    rows = lengths.shape[0]
    return pl.pallas_call(
        table_kernel,
        in_specs=[pl.BlockSpec(memory_space=pltpu.SMEM), pl.BlockSpec(memory_space=pltpu.VMEM)],
        out_shape=[jax.ShapeDtypeStruct((rows, 1, n), jnp.int32) for n in (2 * SPAN, SPAN, SPAN)],
        compiler_params=PARAMS,
        cost_estimate=cost(1, 1),
        name="tables",
    )(place, lengths)


def pack_kernel(count, *refs):
    out_ref = refs[-1]
    pieces, share = out_ref.shape[0], out_ref.shape[-1]
    for t in range(count):
        for f in range(pieces):
            out_ref[f, 0, t] = refs[t][0, 0, :, f * share : (f + 1) * share]


def first_tile(array):
    lead = len(array.shape) - 2
    return pl.BlockSpec((1,) * lead + (16, 128), lambda *_: (0,) * (lead + 2))


def pack(states, chunk, pieces, after=()):
    low, high = chunk
    _, _, piece, width = states[0].shape
    share = width // pieces
    count = len(states)
    shape = (pieces, high - low, count, piece, share)
    return pl.pallas_call(
        lambda *refs: pack_kernel(count, *refs),
        grid=(high - low,),
        in_specs=[
            *[pl.BlockSpec((1, 1, piece, width), lambda r: (0, r + low, 0, 0))] * count,
            *[first_tile(array) for array in after],
        ],
        out_specs=pl.BlockSpec((pieces, 1, count, piece, share), lambda r: (0, r, 0, 0, 0)),
        out_shape=pltpu.HBM(shape, jnp.bfloat16),
        compiler_params=PARAMS,
        cost_estimate=cost(1, 1),
        name="pack",
    )(*[pltpu.with_memory_space_constraint(state, pltpu.HBM) for state in states], *after)


def attend_kernel(side_ref, first_ref, here_ref, ahead_ref, q_ref, next_q_ref, own_ref, other_ref, *refs):
    out_ref, sent_ref, contexts = refs[-3:]
    factor = math.log2(math.e) / math.sqrt(HEAD)
    pieces, _, _, piece, features = q_ref.shape
    block = SPAN // 2

    def rows(ref, index, start, stop, lanes):
        parts = []
        for ring in range(2):
            low, high = max(start - ring * SPAN, 0), min(stop - ring * SPAN, SPAN)
            if low < high:
                some = ref[ring][low // piece : high // piece, 0, index, :, lanes]
                parts.append(some.reshape(high - low, HEAD))
        return parts[0] if len(parts) == 1 else jnp.concatenate(parts, 0)

    def attend_rings(states, queries, spots, keep_at):
        for spot in spots:
            start, stop = max(0, spot - SPAN), spot + block
            key = lax.broadcasted_iota(jnp.int32, (stop - start, block), 0) + start
            here = lax.broadcasted_iota(jnp.int32, (stop - start, block), 1) + spot
            keep = (key >= first_ref[0, :, spot:stop]) & (key <= here)
            bias = jnp.where(keep, 0.0, -1e30)
            for h in range(features // HEAD):
                lanes = slice(h * HEAD, (h + 1) * HEAD)
                scores = dot(rows(states, 0, start, stop, lanes), rows(queries, 0, spot, stop, lanes), NT) + bias
                top = jnp.max(scores, axis=0, keepdims=True)
                raised = jnp.exp2((scores - top) * factor)
                total = jnp.sum(raised, axis=0, keepdims=True)
                weights = (raised * (1.0 / total)).astype(jnp.bfloat16)
                context = dot(weights, rows(states, 1, start, stop, lanes), TN)
                keep_at(slice(spot, stop), lanes, context.astype(jnp.bfloat16))

    @pl.when(side_ref[0] == 0)
    def _():
        def store(at, lanes, context):
            out_ref[0, at.start - SPAN : at.stop - SPAN, lanes] = context

        attend_rings((other_ref, own_ref), (None, q_ref), (SPAN, SPAN + block), store)
        sent_ref[...] = jnp.zeros_like(sent_ref)

    @pl.when(side_ref[0] != 0)
    def _():
        def store(at, lanes, context):
            contexts[at, lanes] = context

        attend_rings((own_ref, other_ref), (q_ref, next_q_ref), (0, block, SPAN, SPAN + block), store)
        source = lax.broadcasted_iota(jnp.int32, (2 * SPAN, SPAN), 0)
        for index, ref in ((here_ref[0], out_ref), (ahead_ref[0], sent_ref)):
            chosen = jnp.where(source == index, 1.0, 0.0).astype(jnp.bfloat16)
            ref[0] = dot(chosen, contexts[...], TN).astype(jnp.bfloat16)


def attend(side, first, here, ahead, q, next_q, own, other, chunk, base, after, weight):
    pieces, _, _, piece, features = own.shape
    low, high = chunk
    rows = high - low

    def line(array):
        return pl.BlockSpec((1, 1, array.shape[2]), lambda r: (r + low, 0, 0))

    def states(array, at):
        return pl.BlockSpec((pieces, 1, array.shape[2], piece, features), lambda r: (0, r + at, 0, 0, 0))

    block = pl.BlockSpec((1, SPAN, features), lambda r: (r, 0, 0))
    return pl.pallas_call(
        attend_kernel,
        grid=(rows,),
        in_specs=[
            pl.BlockSpec(memory_space=pltpu.SMEM),
            line(first),
            line(here),
            line(ahead),
            states(q, low),
            states(next_q, low),
            states(own, low - base),
            states(other, low - base),
            *[first_tile(array) for array in after],
        ],
        out_specs=[block, block],
        out_shape=[jax.ShapeDtypeStruct((rows, SPAN, features), jnp.bfloat16)] * 2,
        scratch_shapes=[pltpu.VMEM((2 * SPAN, features), jnp.bfloat16)],
        compiler_params=pltpu.CompilerParams(vmem_limit_bytes=28 * 2**20),
        cost_estimate=cost(rows * weight, 1),
        name="attend",
    )(side, first, here, ahead, q, next_q, own, other, *after)


def join_kernel(side_ref, mine_ref, other_ref, weight_ref, second_ref, *refs):
    out_ref = refs[-1]
    rows, tokens, depth = mine_ref.shape
    pieces, _, piece, wide = out_ref.shape
    weight = weight_ref[...].reshape(depth, wide)
    second = second_ref[...].reshape(depth, wide)
    for r in range(rows):
        total = dot(mine_ref[r], weight) + dot(other_ref[r], second)
        out_ref[:, r] = total.astype(jnp.bfloat16).reshape(pieces, piece, wide)


def join(side, mine, other, weight, pieces, after=()):
    rows, tokens, depth = mine.shape
    heads, _, head, units = weight.shape
    wide = units // 2
    whole = pl.BlockSpec((rows, tokens, depth), lambda n, side: (0, 0, 0))
    return pl.pallas_call(
        join_kernel,
        grid_spec=pltpu.PrefetchScalarGridSpec(
            num_scalar_prefetch=1,
            grid=(units // wide,),
            in_specs=[
                whole,
                whole,
                pl.BlockSpec((heads, 1, head, wide), lambda n, side: (0, side[0], 0, n)),
                pl.BlockSpec((heads, 1, head, wide), lambda n, side: (0, 1 - side[0], 0, n)),
                *[first_tile(array) for array in after],
            ],
            out_specs=pl.BlockSpec((pieces, rows, tokens // pieces, wide), lambda n, side: (0, 0, 0, n)),
        ),
        out_shape=jax.ShapeDtypeStruct((pieces, rows, tokens // pieces, units), jnp.bfloat16),
        compiler_params=PARAMS,
        cost_estimate=cost(1, 1),
        name="join",
    )(side, mine, other, weight, weight, *after)


def body(queries, key_states, value_vectors, hypothesis_lengths, join_weight):
    _, rows, piece, width = queries.shape
    pieces = SPAN // piece
    share = width // pieces
    side = lax.axis_index("dir")
    ring = lax.axis_index("y") * 8 + lax.axis_index("z")

    def exchange(parts):
        return lax.all_to_all(parts, "x", split_axis=0, concat_axis=0, tiled=True)

    to_left = [(RINGS + c + 1, RINGS + c) for c in range(RINGS - 1)]
    to_right = [(RINGS + c, RINGS + c + 1) for c in range(RINGS - 1)]
    outward = [(c, c + 1) for c in range(RINGS - 1)] + to_left

    def passed(array, pairs):
        return lax.ppermute(array, ("dir", "y", "z"), pairs)

    turned = lax.ppermute(
        join_weight.reshape(piece, -1), ("y", "x"), [(y * 4 + x, x * 4 + y) for y in range(4) for x in range(4)]
    )
    weight = lax.all_gather(turned, ("z", "y"), tiled=True)
    units = weight.shape[1]
    weight_rows = pltpu.with_memory_space_constraint(weight.reshape(share // HEAD, 2, HEAD, units), pltpu.HBM)
    base = (ring - 1 + side) * SPAN
    lines = tables(base[None], hypothesis_lengths)

    both = (key_states, value_vectors)
    own_early = exchange(pack(both, CHUNKS[0], pieces))
    other_early = passed(own_early, outward)
    q = exchange(pack((queries,), (0, rows), pieces, (own_early, turned)))
    next_q = passed(q, to_left)
    own_late = exchange(pack(both, CHUNKS[1], pieces, (q, other_early)))
    other_late = passed(own_late, outward)

    def contexts(own, other, chunk, low, after=(), weight=LONG):
        return attend(side[None], *lines, q, next_q, own, other, chunk, low, after, weight)

    def swapped(mine, ahead):
        mine = mine + passed(ahead, to_right)
        return mine, lax.ppermute(mine, "dir", [(0, 1), (1, 0)])

    def joined_part(mine, partner, after=()):
        return join(side[None], mine, partner, weight_rows, pieces, after)

    def gated(arrived):
        total = jnp.sum(arrived.astype(jnp.float32), axis=0)
        return (jax.nn.silu(total[..., : units // 2]) * total[..., units // 2 :]).astype(jnp.bfloat16)

    early = contexts(own_early, other_early, (0, 2), 0, (own_late,))
    late = contexts(own_late, other_late, (2, 3), 2, (early[1],))
    last = contexts(own_late, other_late, (3, 4), 2, (late[1],))
    early = exchange(joined_part(*swapped(*early), ()))
    late = swapped(*late)
    late = exchange(joined_part(*late, (last[1],)))
    last = exchange(joined_part(*swapped(*last), (early,)))
    joined = [gated(one) for one in (early, late, last)]
    return jnp.concatenate(joined)


def solution(mesh):
    fine = Mesh(mesh.devices.reshape(2, 4, 8, 4), ("dir", "y", "z", "x"))
    states = P("dir", None, ("y", "z", "x"), None)
    return jax.shard_map(
        body,
        mesh=fine,
        in_specs=(states, states, states, P(), P(("y", "z", "x"), None, "dir")),
        out_specs=P(None, ("y", "z", "x"), "dir"),
        check_vma=False,
    )
```
